128 devices in a mesh: dp: 8 (over x_lo, y), ctx: 8 (over x_hi, z), mod: 2 (over core).
Axes of the slice: x: 4 (x_hi: 2, x_lo: 2; x = x_hi * 2 + x_lo), y: 4, z: 4, core: 2. Of those that a mesh axis runs over, the one named last changes fastest.
Arguments:
- hidden_in: bfloat16 [8, 2048, 3584], P('dp', ('ctx', 'mod')), may hold values from -10 to 10
- out_grad: bfloat16 [8, 2048, 1792], P('dp', ('ctx', 'mod')), may hold values from -6 to 6
- modality: int32 [8, 2048], P('dp', ('ctx', 'mod')), may hold values from 0 to 1, as said below
- segment: int32 [8, 2048], P('dp'), may hold values from 0 to 2047, as said below
- w_query: bfloat16 [2, 3584, 1792], P('mod'), may hold values from -1 to 1
- w_keyval: bfloat16 [2, 3584, 512], P('mod'), may hold values from -1 to 1
Outputs:
- attended: bfloat16 [8, 2048, 1792], P('dp', ('ctx', 'mod'))
- grad_hidden: bfloat16 [8, 2048, 3584], P('dp', ('ctx', 'mod'))
- grad_query_w: bfloat16 [2, 3584, 1792], P('mod', ('dp', 'ctx'))
- grad_keyval_w: bfloat16 [2, 3584, 512], P('mod', ('dp', 'ctx'))
The draws below stay inside these ranges and needn't reach their ends.
Inputs may be any that keep to these rules, and one draw needn't show every extreme that they name: Each aligned block of 128 positions holds one modality; the last block of each lane is text. Each position holds the first position of its segment, so it never falls along a lane and starts at 0; every text position starts a segment of its own; a latent segment is a run of whole latent blocks.
All inputs are finite; a program needn't handle non-finite values.
Results may differ from the reference program's by a relative error of at most 0.04.
Values may be sent and summed in bfloat16 or wider, within the bound.
A program may use at most 128 MiB of HBM per device.

```python
import math
import jax
import jax.numpy as jnp
from jax import lax

D = 3584
HS = 128
QH = 14
KVH = 2
BLOCK = 128
QW = 1792
KW = 256
SEQ = 2048
LANES = 8
N_CTX = 8


def block_plan(key):
    block_total = SEQ // BLOCK
    level_key, kind_key, split_key = jax.random.split(key, 3)
    latent_level = jax.random.randint(level_key, (LANES, 1), 1, 8)
    latent = (jax.random.randint(kind_key, (LANES, block_total), 0, 8) < latent_level).astype(jnp.int32)
    not_last = (jnp.arange(block_total, dtype=jnp.int32) < block_total - 1).astype(jnp.int32)[None, :]
    latent = latent * not_last
    split_flag = (jax.random.randint(split_key, (LANES, block_total), 0, 4) == 0).astype(jnp.int32)
    return (latent, split_flag)


def shared_signs(key):
    shared_key = jax.random.fold_in(key, 101)
    direction_key, head_key = jax.random.split(shared_key)
    direction = (2 * jax.random.randint(direction_key, (D,), 0, 2) - 1).astype(jnp.float32) / math.sqrt(D)
    head_signs = (2 * jax.random.randint(head_key, (KVH, HS), 0, 2) - 1).astype(jnp.float32) / math.sqrt(HS)
    return (direction, head_signs)


def draw_modality(key, part):
    latent, split_flag = block_plan(key)
    return jnp.repeat(latent, BLOCK, axis=1).astype(jnp.int32)


def draw_segment(key, part):
    latent, split_flag = block_plan(key)
    earlier = jnp.concatenate([jnp.zeros((LANES, 1), jnp.int32), latent[:, :-1]], axis=1)
    opens = jnp.maximum(1 - earlier, split_flag)
    latent_tok = jnp.repeat(latent, BLOCK, axis=1)
    block_open = jnp.repeat(opens, BLOCK, axis=1)
    positions = jnp.arange(SEQ, dtype=jnp.int32)
    first_tok = (positions % BLOCK == 0)[None, :]
    starts = jnp.where(latent_tok == 0, 1, jnp.where(first_tok, block_open, 0)).astype(jnp.int32)
    marked = jnp.where(starts == 1, positions[None, :], jnp.zeros_like(starts)).astype(jnp.int32)
    return lax.cummax(marked, axis=1).astype(jnp.int32)


def draw_hidden_in(key, part):
    direction, head_signs = shared_signs(key)
    key = jax.random.fold_in(key, 11)
    noise_key, pick_key, level_key = jax.random.split(key, 3)
    noise = jnp.clip(jax.random.normal(noise_key, (LANES, SEQ, D), jnp.float32), -5.0, 5.0)
    level = jax.random.uniform(level_key, (LANES, SEQ, 1), jnp.float32, 10.0, 17.0)
    picked = (jax.random.randint(pick_key, (LANES, SEQ, 1), 0, 48) == 0).astype(jnp.float32)
    strength = picked * level * math.sqrt(math.sqrt(HS))
    return (noise + strength * direction[None, None, :]).astype(jnp.bfloat16)


def draw_w_query(key, part):
    direction, head_signs = shared_signs(key)
    key = jax.random.fold_in(key, 13)
    noise = jnp.clip(jax.random.normal(key, (2, D, QW), jnp.float32), -6.0, 6.0)
    per_group = QH // KVH
    query_line = jnp.broadcast_to(head_signs[:, None, :], (KVH, per_group, HS)).reshape(QW)
    return (noise / math.sqrt(D) + direction[None, :, None] * query_line[None, None, :]).astype(jnp.bfloat16)


def draw_w_keyval(key, part):
    direction, head_signs = shared_signs(key)
    key = jax.random.fold_in(key, 17)
    noise = jnp.clip(jax.random.normal(key, (2, D, 2 * KW), jnp.float32), -6.0, 6.0)
    key_line = jnp.concatenate([head_signs.reshape(KW), jnp.zeros((KW,), jnp.float32)])
    return (noise / math.sqrt(D) + direction[None, :, None] * key_line[None, None, :]).astype(jnp.bfloat16)


def block_levels(stream_key, dims, pieces, smallest, top_value):
    gain, own = 1.0, jax.random.fold_in(stream_key, 6)
    for position, blocks in pieces:
        steps = jnp.exp(jax.random.uniform(jax.random.fold_in(own, position), (blocks,), jnp.float32, smallest / len(pieces), top_value / len(pieces)))
        gain = gain * jnp.repeat(steps, dims[position] // blocks).reshape([-1 if axis == position else 1 for axis in range(len(dims))])
    return gain


def scatter_about(rng, extent, width, reach, cuts=(), kind=jnp.bfloat16):
    entries = width * jax.random.normal(rng, extent, jnp.float32)
    if cuts:
        entries = entries * block_levels(rng, extent, cuts, -0.22, 0.18)
    return jnp.clip(entries, -reach, reach).astype(kind)


def setup_inputs(seed: int = 0) -> dict:
    streams_of = jax.random.split(jax.random.key(seed), 7)
    return {
        "hidden_in": draw_hidden_in(jax.random.fold_in(streams_of[6], 71), 0),
        "out_grad": scatter_about(streams_of[1], (LANES, SEQ, QW), 1.0, 6.0, ((0, 8), (1, 16))),
        "modality": draw_modality(jax.random.fold_in(streams_of[6], 71), 0),
        "segment": draw_segment(jax.random.fold_in(streams_of[6], 71), 0),
        "w_query": draw_w_query(jax.random.fold_in(streams_of[6], 71), 0),
        "w_keyval": draw_w_keyval(jax.random.fold_in(streams_of[6], 71), 0),
    }


masked_low = -1e+30

def lane_pass(inputs, w_both):
    tokens, cotangent, kinds, segs = inputs
    score_scale = 1.0 / math.sqrt(HS)
    per_group = QH // KVH
    first = jnp.dot(tokens, w_both[0], preferred_element_type=jnp.float32)
    second = jnp.dot(tokens, w_both[1], preferred_element_type=jnp.float32)
    projected = jnp.where(kinds[:, None] == 1, second, first).astype(jnp.bfloat16)
    queries = projected[:, :QW].reshape(SEQ, KVH, per_group, HS).astype(jnp.float32)
    keys = projected[:, QW:QW + KW].reshape(SEQ, KVH, HS).astype(jnp.float32)
    values = projected[:, QW + KW:].reshape(SEQ, KVH, HS).astype(jnp.float32)
    scores = jnp.einsum('rgjd,ngd->gjrn', queries, keys) * score_scale
    allowed = segs[None, :] <= segs[:, None]
    row_top = lax.optimization_barrier(jnp.max(jnp.where(allowed, scores, masked_low), axis=-1))
    weights = jnp.where(allowed, jnp.exp(scores - row_top[..., None]), 0.0)
    weight_sum = lax.optimization_barrier(jnp.sum(weights, axis=-1))
    weighted = jnp.einsum('gjrn,ngd->gjrd', weights.astype(jnp.bfloat16).astype(jnp.float32), values)
    attended = jnp.transpose(weighted / weight_sum[..., None], (2, 0, 1, 3)).reshape(SEQ, QW).astype(jnp.bfloat16)
    log_total = row_top + jnp.log(weight_sum)
    grad_out = cotangent.reshape(SEQ, KVH, per_group, HS).astype(jnp.float32)
    delta = jnp.einsum('rgjd,rgjd->gjr', grad_out, attended.reshape(SEQ, KVH, per_group, HS).astype(jnp.float32))
    prob = jnp.where(allowed, jnp.exp(scores - log_total[..., None]), 0.0)
    dprob = jnp.einsum('rgjd,ngd->gjrn', grad_out, values)
    dscore = (prob * (dprob - delta[..., None])).astype(jnp.bfloat16).astype(jnp.float32)
    grad_q = (jnp.einsum('gjrn,ngd->rgjd', dscore, keys) * score_scale).astype(jnp.bfloat16)
    grad_k = (jnp.einsum('gjrn,rgjd->ngd', dscore, queries) * score_scale).astype(jnp.bfloat16)
    grad_v = jnp.einsum('gjrn,rgjd->ngd', prob.astype(jnp.bfloat16).astype(jnp.float32), grad_out).astype(jnp.bfloat16)
    grads = jnp.concatenate([grad_q.reshape(SEQ, QW), grad_k.reshape(SEQ, KW), grad_v.reshape(SEQ, KW)], axis=1)
    back_first = jnp.dot(grads, w_both[0].T, preferred_element_type=jnp.float32)
    back_second = jnp.dot(grads, w_both[1].T, preferred_element_type=jnp.float32)
    grad_hidden = jnp.where(kinds[:, None] == 1, back_second, back_first).astype(jnp.bfloat16)
    return (attended, grad_hidden, grads)

def reference(hidden_in, out_grad, modality, segment, w_query, w_keyval):
    w_both = jnp.concatenate([w_query, w_keyval], axis=2)
    attended, grad_hidden, grads = lax.map(lambda inputs: lane_pass(inputs, w_both), (hidden_in, out_grad, modality, segment))
    part_rows = SEQ // N_CTX
    grad_cols = QW + 2 * KW
    tok_parts = hidden_in.reshape(LANES, N_CTX, part_rows, D)
    grad_parts = grads.reshape(LANES, N_CTX, part_rows, grad_cols)
    kind_parts = modality.reshape(LANES, N_CTX, part_rows)

    def one_part(running, part_index):
        tok_rows = tok_parts[:, part_index]
        grad_rows = grad_parts[:, part_index].astype(jnp.float32)
        kind_rows = kind_parts[:, part_index]
        sums = []
        for expert in range(2):
            chosen = jnp.where(kind_rows[..., None] == expert, tok_rows, jnp.zeros_like(tok_rows)).astype(jnp.float32)
            piece = jnp.einsum('lrd,lrc->ldc', chosen, grad_rows)
            piece = piece.astype(jnp.bfloat16).astype(jnp.float32)
            sums.append(lax.optimization_barrier(jnp.sum(piece, axis=0)))
        return (running + jnp.stack(sums), None)
    totals, unused = lax.scan(one_part, jnp.zeros((2, D, grad_cols), jnp.float32), jnp.arange(N_CTX, dtype=jnp.int32))
    totals = totals.astype(jnp.bfloat16)
    return (attended, grad_hidden, totals[:, :, :QW], totals[:, :, QW:])
```

```python
import functools
import math

import jax
import jax.numpy as jnp
from jax import lax
from jax.experimental import pallas as pl
from jax.experimental.pallas import tpu as pltpu
from jax.sharding import PartitionSpec as P

HS = 128
BLOCK = 128
D = 3584
QW = 1792
KW = 256
SEQ = 2048
HEADS = 7
GW = HEADS * HS
CHIP = 2 * BLOCK
SLICE = 448
PART = 56
MESH = pl.DeviceIdType.MESH
BF = jnp.bfloat16
F32 = jnp.float32


def aligned(index, step):
    return pl.multiple_of(index * step, step)


def dot(a, b, dims=((1,), (0,))):
    return lax.dot_general(a, b, (dims, ((), ())), preferred_element_type=F32)


def send(src, dst, send_sem, recv_sem, **device):
    return pltpu.make_async_remote_copy(
        src_ref=src, dst_ref=dst, send_sem=send_sem, recv_sem=recv_sem,
        device_id=device, device_id_type=MESH,
    )


def arrived(dst, sem):
    pltpu.make_async_copy(dst, dst, sem).wait()


def layer(
    hid, og, modv, segv, wq, wkv,
    att_o, gh_o, gwq_o, gwkv_o,
    wq_v, wkv_v, hidf, hid_t, ogf, mods, at, kvs, kvr, kvall, qs, qr, qf, bias,
    attb, attf, dqb, gq, acc, dkvb, dkr, dkx, dkxr, gkv, bg, be, cf, cs, crz, cx, cxr, keep, fin, finr, sb, sr,
    w_sem, pair_s, pair_r, mod_s, mod_r, a_s, a_r, af_s, af_r, kv_s, kv_r,
    att_s, att_r, gq_s, gq_r, b_s, b_r, dk_s, dk_r, c_s, c_r, cx_s, cx_r, fin_s, fin_r,
):
    dp, ctx, core = lax.axis_index("dp"), lax.axis_index("ctx"), lax.axis_index("mod")
    xlo, y, xhi, z = dp // 4, dp % 4, ctx // 4, ctx % 4
    other = 1 - core
    here = dp * 2 + core
    expert = core.astype(F32)
    scale = 1.0 / math.sqrt(HS)

    q_cols = []
    for group in (other, core):
        for first, width in ((0, 512), (512, 384)):
            q_cols.append((group, first, width))
    loads = [pltpu.make_async_copy(wkv, wkv_v, w_sem.at[0])]
    for i, (group, first, width) in enumerate(q_cols):
        cols = pl.ds(pl.multiple_of(group * GW + first, 128), width)
        loads.append(pltpu.make_async_copy(wq.at[:, cols], wq_v.at[:, cols], w_sem.at[1 + i]))
    for load in loads:
        load.start()

    barrier = pltpu.get_barrier_semaphore()
    for k in range(8):
        pl.semaphore_signal(barrier, inc=1, device_id={"dp": (dp + k) % 8, "mod": other}, device_id_type=MESH)
        if k:
            pl.semaphore_signal(barrier, inc=1, device_id={"dp": (dp + k) % 8}, device_id_type=MESH)
            pl.semaphore_signal(barrier, inc=1, device_id={"ctx": (ctx + k) % 8}, device_id_type=MESH)
    pl.semaphore_wait(barrier, 22)

    own_rows = pl.ds(aligned(core, BLOCK), BLOCK)
    other_rows = pl.ds(aligned(other, BLOCK), BLOCK)
    sent = []

    hid_copy = send(hid, hidf.at[own_rows], pair_s.at[0], pair_r.at[0], mod=other)
    hid_copy.start()
    og_copy = send(og.at[:, pl.ds(aligned(other, GW), GW)], ogf.at[own_rows], pair_s.at[1], pair_r.at[1], mod=other)
    og_copy.start()
    sent += [hid_copy, og_copy]
    mods[here] = modv[...]
    for k in range(8):
        for c in range(2):
            if k == 0 and c == 0:
                continue
            dev = {"dp": (dp + k) % 8, "mod": other if c else core}
            copy = send(modv, mods.at[here], mod_s.at[k, c], mod_r.at[k, c], **dev)
            copy.start()
            sent.append(copy)
    hidf[own_rows, :] = hid[...]
    ogf[own_rows, :] = og[:, pl.ds(aligned(core, GW), GW)]

    here_lanes = pl.ds(aligned(here, BLOCK), BLOCK)
    for i in range(7):
        hid_t[i * 512:(i + 1) * 512, :] = hid[:, i * 512:(i + 1) * 512].T
    for k in (5, 1, 6, 3, 4, 2, 7):
        to = (dp + k) % 8
        for s in range(2):
            rows = pl.ds(pl.multiple_of((s * 4 + to % 4) * SLICE, 64), SLICE)
            copy = send(
                hid_t.at[rows], at.at[pl.ds(s * SLICE, SLICE), here_lanes], a_s.at[k, s], a_r.at[k, s], dp=to
            )
            copy.start()
            sent.append(copy)
    for s in range(2):
        rows = pl.ds(pl.multiple_of((s * 4 + y) * SLICE, 64), SLICE)
        at[s * SLICE:(s + 1) * SLICE, here_lanes] = hid_t[rows, :]

    hid_copy.wait_recv()
    loads[0].wait()
    made = dot(hidf[...], wkv_v[...]).astype(BF)
    for i in range(2):
        for g in range(2):
            kvs[i, g] = made[:, (i * 2 + g) * HS:(i * 2 + g + 1) * HS]
    copy = send(kvs.at[:, other], kvr, pair_s.at[2], pair_r.at[2], mod=other)
    copy.start()
    sent.append(copy)
    for k in range(8):
        for c in range(2):
            if k or c:
                arrived(mods.at[(dp - k + 8) % 8 * 2 + (other if c else core)], mod_r.at[k, c])
    mine = [
        jnp.broadcast_to(mods[dp * 2 + b][0:1, :], (BLOCK, HS)) == expert for b in range(2)
    ]
    copy.wait_recv()
    for i in range(2):
        for b in range(2):
            rows = slice(b * BLOCK, (b + 1) * BLOCK)
            kvall[i, pl.ds(pl.multiple_of(ctx * CHIP + b * BLOCK, BLOCK), BLOCK), :] = jnp.where(
                mine[b], kvs[i, core, rows, :], kvr[i, rows, :]
            )
    ctx_rows = pl.ds(aligned(ctx, CHIP), CHIP)
    xctx = (1 - xhi) * 4 + z
    xctx_rows = pl.ds(aligned(xctx, CHIP), CHIP)
    copy = send(kvall.at[:, ctx_rows], kvall.at[:, ctx_rows], kv_s.at[0, 0], kv_r.at[0, 0], ctx=xctx)
    copy.start()
    sent.append(copy)
    for k in (1, 3, 2):
        copy = send(
            kvall.at[:, ctx_rows], kvall.at[:, ctx_rows], kv_s.at[0, k], kv_r.at[0, k], ctx=xhi * 4 + (z + k) % 4
        )
        copy.start()
        sent.append(copy)

    def project(i):
        group, first, width = q_cols[i]
        loads[1 + i].wait()
        cols = pl.ds(pl.multiple_of(group * GW + first, 128), width)
        qs[group, :, first:first + width] = dot(hidf[...], wq_v[:, cols]).astype(BF)

    project(0)
    arrived(kvall.at[:, xctx_rows], kv_r.at[0, 0])
    for k in (1, 3, 2):
        copy = send(
            kvall.at[:, xctx_rows], kvall.at[:, xctx_rows], kv_s.at[1, k], kv_r.at[1, k], ctx=xhi * 4 + (z + k) % 4
        )
        copy.start()
        sent.append(copy)
    project(1)
    q_copy = send(qs.at[other], qr, pair_s.at[3], pair_r.at[3], mod=other)
    q_copy.start()
    sent.append(q_copy)
    project(2)
    project(3)
    seg_rows = segv[:, pl.ds(aligned(ctx, CHIP), CHIP)]
    seg_col = jnp.broadcast_to(seg_rows[0:1, :], (128, CHIP)).T[:, 0:1]
    bias[...] = jnp.where(segv[0:1, :] <= seg_col, 0.0, -1e30)
    acc[...] = jnp.zeros_like(acc)
    q_copy.wait_recv()
    for b in range(2):
        rows = slice(b * BLOCK, (b + 1) * BLOCK)
        pick = jnp.broadcast_to(mods[dp * 2 + b][0:1, 0:1], (BLOCK, GW)) == expert
        qf[rows, :] = jnp.where(pick, qs[core, rows, :], qr[rows, :])
    og_copy.wait_recv()
    for k in (1, 3, 2):
        for part, half in enumerate((xhi, 1 - xhi)):
            rows = pl.ds(aligned(half * 4 + (z - k + 4) % 4, CHIP), CHIP)
            arrived(kvall.at[:, rows], kv_r.at[part, k])

    def forward_hidden(k):
        lanes = pl.ds(pl.multiple_of(((dp - k + 8) % 8 * 2 + core) * BLOCK, BLOCK), BLOCK)
        copy = send(at.at[:, lanes], at.at[:, lanes], af_s.at[k], af_r.at[k], mod=other)
        return copy

    def one_head(i, carry):
        slot, target = i // 2, i % 2
        head = target * 4 + slot
        lanes = pl.ds(aligned(head, HS), HS)
        full_lanes = pl.ds(aligned(core * HEADS + head, HS), HS)
        q, go = qf[:, lanes], ogf[:, lanes]
        keys, values = kvall[0], kvall[1]
        scores = dot(q, keys, ((1,), (1,))) * (scale * math.log2(math.e)) + bias[...]
        top = jnp.max(scores, axis=1, keepdims=True)
        weights = jnp.exp2(scores - top)
        total = jnp.sum(weights, axis=1, keepdims=True)
        low = weights.astype(BF)
        inv = 1.0 / total
        attended = (dot(low, values) * inv).astype(BF)
        attb[head] = attended
        copy = send(
            attb.at[head, other_rows], attf.at[:, full_lanes], att_s.at[head], att_r.at[head], mod=other
        )
        copy.start()
        attf[:, full_lanes] = attb[head, own_rows, :]
        go32 = go.astype(F32)
        delta = jnp.sum(go32 * attended.astype(F32), axis=1, keepdims=True)
        dprob = dot(go, values, ((1,), (1,)))
        dscore = (weights * (dprob * inv - delta * inv)).astype(BF)
        dq = (dot(dscore, keys) * scale).astype(BF)
        dqb[head] = dq
        gq[:, full_lanes] = dq
        copy = send(dqb.at[head], gq.at[:, full_lanes], gq_s.at[head], gq_r.at[head], mod=other)
        copy.start()
        send_grads(dqb.at[head], target, slot, b_s.at[head])
        acc[0] += dot(q.T, dscore)
        acc[1] += dot((go32 * inv).astype(BF).T, low)
        return carry

    def grads_copy(src, target, slot, sems, k):
        rows = pl.ds(aligned(dp, CHIP), CHIP)
        return send(
            src, bg.at[slot, rows], sems.at[k], b_r.at[slot, dp], dp=core * 4 + (y + k) % 4, mod=target
        )

    def send_grads(src, target, slot, sems):
        at_home = jnp.logical_and(xlo == core, target == core)
        rows = pl.ds(aligned(dp, CHIP), CHIP)
        for k in (1, 3, 2):
            grads_copy(src, target, slot, sems, k).start()

        @pl.when(at_home)
        def _():
            pltpu.make_async_copy(src, bg.at[slot, rows], b_r.at[slot, dp]).start()

        @pl.when(jnp.logical_not(at_home))
        def _():
            grads_copy(src, target, slot, sems, 0).start()

    def grads_sent(src, target, slot, sems):
        at_home = jnp.logical_and(xlo == core, target == core)
        for k in (1, 3, 2):
            grads_copy(src, target, slot, sems, k).wait_send()

        @pl.when(jnp.logical_not(at_home))
        def _():
            grads_copy(src, target, slot, sems, 0).wait_send()

    lax.fori_loop(0, 4, one_head, 0)
    for k in range(8):
        if k:
            lanes = pl.ds(pl.multiple_of(((dp - k + 8) % 8 * 2 + core) * BLOCK, BLOCK), BLOCK)
            for s in range(2):
                arrived(at.at[pl.ds(s * SLICE, SLICE), lanes], a_r.at[k, s])
        copy = forward_hidden(k)
        copy.start()
        sent.append(copy)
    lax.fori_loop(4, HEADS, one_head, 0)

    for c in range(8):
        for i in range(2):
            dkvb[c // 4, c % 4, i] = acc[i, :, c * CHIP:(c + 1) * CHIP].astype(BF)
    for k in (1, 3, 2):
        to = (z + k) % 4
        copy = send(dkvb.at[:, to], dkr.at[k - 1], dk_s.at[k], dk_r.at[k], ctx=xhi * 4 + to)
        copy.start()
        sent.append(copy)

    for k in range(8):
        lanes = pl.ds(pl.multiple_of(((dp - k + 8) % 8 * 2 + other) * BLOCK, BLOCK), BLOCK)
        arrived(at.at[:, lanes], af_r.at[k])

    def weight_block(slot, carry):
        for source in range(8):
            arrived(bg.at[slot, pl.ds(source * CHIP, CHIP)], b_r.at[slot, source])
        for t in range(16):
            rows = slice(t * BLOCK, (t + 1) * BLOCK)
            kind = mods[t][0:1, :]
            block = bg[slot, rows, :]
            second = jnp.where(jnp.broadcast_to(kind, (BLOCK, HS)) == 1.0, block, jnp.zeros_like(block))
            be[rows, HS:] = second
            be[rows, :HS] = block - second
        cf[...] = dot(at[...], be[...])
        for c in range(8):
            for e in range(2):
                cols = slice(e * HS, (e + 1) * HS)
                both = jnp.concatenate(
                    [cf[c * PART:(c + 1) * PART, cols], cf[SLICE + c * PART:SLICE + (c + 1) * PART, cols]], axis=0
                )
                cs[slot, c % 4, c // 4, e] = both.astype(BF)
        for k in (1, 3, 2):
            to = (z + k) % 4
            send(cs.at[slot, to], crz.at[slot, k - 1], c_s.at[slot, k], c_r.at[slot, k], ctx=xhi * 4 + to).start()
        return carry

    lax.fori_loop(0, 3, weight_block, 0)

    for k in (1, 3, 2):
        arrived(dkr.at[k - 1], dk_r.at[k])

    def over_z(half):
        lanes = pl.ds(pl.multiple_of((half * 4 + z) * CHIP, CHIP), CHIP)
        out = []
        for i in range(2):
            total = acc[i, :, lanes]
            for k in range(3):
                total += dkr[k, half, i].astype(F32)
            out.append(total)
        return out

    for i, total in enumerate(over_z(1 - xhi)):
        dkx[i] = total.astype(BF)
    copy = send(dkx, dkxr, dk_s.at[0], dk_r.at[0], ctx=xctx)
    copy.start()
    sent.append(copy)
    kept = over_z(xhi)
    copy.wait_recv()
    for i in range(2):
        total = (kept[i] + dkxr[i].astype(F32)) * (scale if i == 0 else 1.0)
        gkv[i, core] = total.T.astype(BF)
    gkv_copy = send(gkv.at[:, core], gkv.at[:, core], pair_s.at[4], pair_r.at[4], mod=other)
    gkv_copy.start()
    sent.append(gkv_copy)
    send_grads(gkv.at[0, core], 0, 4, b_s.at[7])
    send_grads(gkv.at[1, core], 1, 3, b_s.at[8])

    for head in range(HEADS):
        arrived(gq.at[:, pl.ds(aligned(other * HEADS + head, HS), HS)], gq_r.at[head])
    arrived(gkv.at[:, other], pair_r.at[4])

    def spread(i, carry):
        rows = pl.ds(aligned(i, 512), 512)
        grads_kv = jnp.concatenate([gkv[0, 0], gkv[0, 1], gkv[1, 0], gkv[1, 1]], axis=1)
        total = dot(gq[...], wq_v[rows, :], ((1,), (1,))) + dot(grads_kv, wkv_v[rows, :], ((1,), (1,)))
        sb[:, rows] = total.astype(BF)
        return carry

    lax.fori_loop(0, 7, spread, 0)
    home_copy = send(sb.at[other_rows], sr, pair_s.at[5], pair_r.at[5], mod=other)
    home_copy.start()
    sent.append(home_copy)

    last = 5 - core
    lax.fori_loop(3, last, weight_block, 0)

    def sum_z(slot, carry):
        for k in (1, 3, 2):
            arrived(crz.at[slot, k - 1], c_r.at[slot, k])
        for e in range(2):
            for half, far in ((1 - xhi, True), (xhi, False)):
                total = cs[slot, z, half, e].astype(F32)
                for k in range(3):
                    total += crz[slot, k, half, e].astype(F32)
                if far:
                    cx[slot, e] = total.astype(BF)
                else:
                    keep[slot, e] = total
        send(cx.at[slot], cxr.at[slot], cx_s.at[slot], cx_r.at[slot], ctx=xctx).start()
        return carry

    lax.fori_loop(0, last, sum_z, 0)
    fin[...] = jnp.zeros_like(fin)

    def sum_x(slot, carry):
        arrived(cxr.at[slot], cx_r.at[slot])
        for e in range(2):
            total = keep[slot, e] + cxr[slot, e].astype(F32)
            for s in range(2):
                padded = jnp.concatenate([total[s * PART:(s + 1) * PART], jnp.zeros((8, HS), F32)], axis=0)
                fin[s, e, slot] = padded.astype(BF)
        return carry

    lax.fori_loop(0, last, sum_x, 0)
    for s in range(2):
        for e in range(2):
            at_home = jnp.logical_and(xlo == s, core == e)
            copy = send(
                fin.at[s, e], finr.at[xlo, core], fin_s.at[s, e], fin_r.at[xlo, core], dp=s * 4 + y, mod=e
            )

            @pl.when(at_home)
            def _():
                pltpu.make_async_copy(fin.at[s, e], finr.at[xlo, core], fin_r.at[xlo, core]).start()

            @pl.when(jnp.logical_not(at_home))
            def _():
                copy.start()

    for head in range(HEADS):
        lanes = pl.ds(aligned(other * HEADS + head, HS), HS)
        arrived(attf.at[:, lanes], att_r.at[head])
    att_o[...] = attf[...]
    arrived(sr, pair_r.at[5])
    pick = jnp.broadcast_to(mods[here][0:1, 0:1], (BLOCK, D)) == expert
    gh_o[...] = jnp.where(pick, sb[own_rows, :], sr[...])

    for g in range(2):
        for c in range(2):
            arrived(finr.at[g, c], fin_r.at[g, c])
    for g in range(2):
        for head in range(HEADS):
            cols = slice((g * HEADS + head) * HS, (g * HEADS + head + 1) * HS)
            gwq_o[:, cols] = finr[g, head // 4, head % 4][:PART]
        gwkv_o[:, g * HS:(g + 1) * HS] = finr[g, 0, 4][:PART]
        gwkv_o[:, KW + g * HS:KW + (g + 1) * HS] = finr[g, 1, 3][:PART]

    for copy in sent:
        copy.wait_send()

    def heads_sent(head, carry):
        full_lanes = pl.ds(aligned(core * HEADS + head, HS), HS)
        send(
            attb.at[head, other_rows], attf.at[:, full_lanes], att_s.at[head], att_r.at[head], mod=other
        ).wait_send()
        send(dqb.at[head], gq.at[:, full_lanes], gq_s.at[head], gq_r.at[head], mod=other).wait_send()
        grads_sent(dqb.at[head], head // 4, head % 4, b_s.at[head])
        return carry

    lax.fori_loop(0, HEADS, heads_sent, 0)
    grads_sent(gkv.at[0, core], 0, 4, b_s.at[7])
    grads_sent(gkv.at[1, core], 1, 3, b_s.at[8])

    def blocks_sent(slot, carry):
        for k in (1, 3, 2):
            to = (z + k) % 4
            send(cs.at[slot, to], crz.at[slot, k - 1], c_s.at[slot, k], c_r.at[slot, k], ctx=xhi * 4 + to).wait_send()
        send(cx.at[slot], cxr.at[slot], cx_s.at[slot], cx_r.at[slot], ctx=xctx).wait_send()
        return carry

    lax.fori_loop(0, last, blocks_sent, 0)
    for s in range(2):
        for e in range(2):
            copy = send(
                fin.at[s, e], finr.at[xlo, core], fin_s.at[s, e], fin_r.at[xlo, core], dp=s * 4 + y, mod=e
            )

            @pl.when(jnp.logical_not(jnp.logical_and(xlo == s, core == e)))
            def _():
                copy.wait_send()


def on_device(hidden_in, out_grad, modality, segment, w_query, w_keyval):
    vmem, dma = pltpu.VMEM, pltpu.SemaphoreType.DMA
    scratch = [
        vmem((D, QW), BF), vmem((D, 2 * KW), BF),
        vmem((CHIP, D), BF), vmem((D, BLOCK), BF), vmem((CHIP, GW), BF), vmem((16, 8, HS), F32),
        vmem((2 * SLICE, SEQ), BF),
        vmem((2, 2, CHIP, HS), BF), vmem((2, CHIP, HS), BF), vmem((2, SEQ, HS), BF),
        vmem((2, CHIP, GW), BF), vmem((CHIP, GW), BF), vmem((CHIP, GW), BF), vmem((CHIP, SEQ), F32),
        vmem((HEADS, CHIP, HS), BF), vmem((BLOCK, QW), BF), vmem((HEADS, CHIP, HS), BF), vmem((CHIP, QW), BF),
        vmem((2, HS, SEQ), F32), vmem((2, 4, 2, HS, CHIP), BF), vmem((3, 2, 2, HS, CHIP), BF),
        vmem((2, HS, CHIP), BF), vmem((2, HS, CHIP), BF), vmem((2, 2, CHIP, HS), BF),
        vmem((5, SEQ, HS), BF), vmem((SEQ, 2 * HS), BF), vmem((2 * SLICE, 2 * HS), F32),
        vmem((5, 4, 2, 2, 2 * PART, HS), BF), vmem((5, 3, 2, 2, 2 * PART, HS), BF),
        vmem((5, 2, 2 * PART, HS), BF), vmem((5, 2, 2 * PART, HS), BF), vmem((5, 2, 2 * PART, HS), F32),
        vmem((2, 2, 5, 64, HS), BF), vmem((2, 2, 5, 64, HS), BF),
        vmem((CHIP, D), BF), vmem((BLOCK, D), BF),
        dma((5,)), dma((6,)), dma((6,)), dma((8, 2)), dma((8, 2)), dma((8, 2)), dma((8, 2)), dma((8,)), dma((8,)),
        dma((2, 4)), dma((2, 4)), dma((HEADS,)), dma((HEADS,)), dma((HEADS,)), dma((HEADS,)),
        dma((9, 4)), dma((5, 8)), dma((4,)), dma((4,)), dma((5, 4)), dma((5, 4)), dma((5,)), dma((5,)),
        dma((2, 2)), dma((2, 2)),
    ]
    in_vmem, anywhere = pl.BlockSpec(memory_space=pltpu.VMEM), pl.BlockSpec(memory_space=pl.ANY)
    kinds = jnp.broadcast_to(modality.astype(F32), (8, BLOCK))
    segs = jnp.broadcast_to(segment.astype(F32), (8, SEQ))
    attended, grad_hidden, grad_wq, grad_wkv = pl.pallas_call(
        layer,
        out_shape=(
            jax.ShapeDtypeStruct((BLOCK, QW), BF),
            jax.ShapeDtypeStruct((BLOCK, D), BF),
            jax.ShapeDtypeStruct((PART, QW), BF),
            jax.ShapeDtypeStruct((PART, 2 * KW), BF),
        ),
        in_specs=[in_vmem] * 4 + [anywhere] * 2,
        out_specs=(in_vmem,) * 4,
        scratch_shapes=scratch,
        compiler_params=pltpu.CompilerParams(
            collective_id=0, has_side_effects=True, vmem_limit_bytes=63 * 2**20
        ),
        name="layer",
    )(hidden_in[0], out_grad[0], kinds, segs, w_query[0], w_keyval[0])
    return attended[None], grad_hidden[None], grad_wq[None], grad_wkv[None]


def solution(mesh):
    return jax.shard_map(
        on_device,
        mesh=mesh,
        in_specs=(
            P("dp", ("ctx", "mod"), None),
            P("dp", ("ctx", "mod"), None),
            P("dp", ("ctx", "mod")),
            P("dp", None),
            P("mod", None, None),
            P("mod", None, None),
        ),
        out_specs=(
            P("dp", ("ctx", "mod"), None),
            P("dp", ("ctx", "mod"), None),
            P("mod", ("dp", "ctx"), None),
            P("mod", ("dp", "ctx"), None),
        ),
        check_vma=False,
    )
```

```python
import functools
import math

import jax
import jax.numpy as jnp
from jax import lax
from jax.experimental import pallas as pl
from jax.experimental.pallas import tpu as pltpu
from jax.sharding import PartitionSpec as P

HS = 128
BLOCK = 128
D = 3584
QW = 1792
KW = 256
SEQ = 2048
HEADS = 7
GW = HEADS * HS
CHIP = 2 * BLOCK
SLICE = 448
PART = 56
LAG = 2
MESH = pl.DeviceIdType.MESH
BF = jnp.bfloat16
F32 = jnp.float32


def aligned(index, step):
    return pl.multiple_of(index * step, step)


def dot(a, b, dims=((1,), (0,))):
    return lax.dot_general(a, b, (dims, ((), ())), preferred_element_type=F32)


def send(src, dst, send_sem, recv_sem, **device):
    return pltpu.make_async_remote_copy(
        src_ref=src, dst_ref=dst, send_sem=send_sem, recv_sem=recv_sem,
        device_id=device, device_id_type=MESH,
    )


def arrived(dst, sem):
    pltpu.make_async_copy(dst, dst, sem).wait()


def layer(
    hid_h, og_h, kinds, segs, wq, wkv,
    attf, gh_o, finr,
    hid, og, wq_v, wkv_v, hidf, hid_t, ogf, mods, at, kvs, kvr, kvall, qs, qr, qf, bias,
    modv, attb, dqb, dqx, gq, acc, dkvb, dkr, dvr, dvz, dvzr, dkx, dkxr, gkv, gkvx, bg, be, cf, cs, cs1, crz, crx, cx, cxr, cz, czr, keep, fin, sb, sr,
    w_sem, pair_s, pair_r, mod_s, mod_r, a_s, a_r, af_s, af_r, kv_s, kv_r,
    att_s, att_r, gq_s, gq_r, bx_s, bx_r, b_s, b_r, dk_s, dk_r, c_s, c_r, cx_s, cx_r, fin_s, fin_r,
):
    dp, ctx, core = lax.axis_index("dp"), lax.axis_index("ctx"), lax.axis_index("mod")
    xlo, y, xhi, z = dp // 4, dp % 4, ctx // 4, ctx % 4
    other = 1 - core
    here = dp * 2 + core
    expert = core.astype(F32)
    scale = 1.0 / math.sqrt(HS)

    q_cols = []
    for group in (other, core):
        for first, width in ((0, 512), (512, 384)):
            q_cols.append((group, first, width))
    own_loads = [
        pltpu.make_async_copy(hid_h, hid, w_sem.at[5]), pltpu.make_async_copy(og_h, og, w_sem.at[6])
    ]
    loads = [pltpu.make_async_copy(wkv, wkv_v, w_sem.at[0])]
    for i, (group, first, width) in enumerate(q_cols):
        cols = pl.ds(pl.multiple_of(group * GW + first, 128), width)
        loads.append(pltpu.make_async_copy(wq.at[:, cols], wq_v.at[:, cols], w_sem.at[1 + i]))
    barrier = pltpu.get_barrier_semaphore()
    for k in range(8):
        pl.semaphore_signal(barrier, inc=1, device_id={"dp": (dp + k) % 8, "mod": other}, device_id_type=MESH)
        if k:
            pl.semaphore_signal(barrier, inc=1, device_id={"dp": (dp + k) % 8}, device_id_type=MESH)
            pl.semaphore_signal(barrier, inc=1, device_id={"ctx": (ctx + k) % 8}, device_id_type=MESH)
    for load in own_loads + loads:
        load.start()
    for load in own_loads:
        load.wait()
    pl.semaphore_wait(barrier, 22)

    own_rows = pl.ds(aligned(core, BLOCK), BLOCK)
    other_rows = pl.ds(aligned(other, BLOCK), BLOCK)
    sent = []

    hid_copy = send(hid, hidf.at[own_rows], pair_s.at[0], pair_r.at[0], mod=other)
    hid_copy.start()
    og_copy = send(og.at[:, pl.ds(aligned(other, GW), GW)], ogf.at[own_rows], pair_s.at[1], pair_r.at[1], mod=other)
    og_copy.start()
    sent += [hid_copy, og_copy]
    modv[...] = jnp.broadcast_to(kinds[...].astype(F32), (8, BLOCK))
    mods[here] = modv[...]
    for k in range(8):
        for c in range(2):
            if k == 0 and c == 0:
                continue
            dev = {"dp": (dp + k) % 8, "mod": other if c else core}
            copy = send(modv, mods.at[here], mod_s.at[k, c], mod_r.at[k, c], **dev)
            copy.start()
            sent.append(copy)
    hidf[own_rows, :] = hid[...]
    ogf[own_rows, :] = og[:, pl.ds(aligned(core, GW), GW)]

    here_lanes = pl.ds(aligned(here, BLOCK), BLOCK)
    for i in range(7):
        hid_t[i * 512:(i + 1) * 512, :] = hid[:, i * 512:(i + 1) * 512].T
    def send_hidden(side, k):
        to = (y + k) % 4
        for s in range(2):
            rows = pl.ds(pl.multiple_of((s * 4 + to) * SLICE, 64), SLICE)
            copy = send(
                hid_t.at[rows], at.at[pl.ds(s * SLICE, SLICE), here_lanes], a_s.at[side, k, s], a_r.at[side, k, s],
                dp=(xlo if side == 0 else 1 - xlo) * 4 + to,
            )
            copy.start()
            sent.append(copy)

    for side, k in ((1, 0), (0, 1), (0, 3), (0, 2)):
        send_hidden(side, k)
    for s in range(2):
        rows = pl.ds(pl.multiple_of((s * 4 + y) * SLICE, 64), SLICE)
        at[s * SLICE:(s + 1) * SLICE, here_lanes] = hid_t[rows, :]

    def lanes_of(side, k):
        return pl.ds(pl.multiple_of((((xlo if side == 0 else 1 - xlo) * 4 + (y - k + 4) % 4) * 2 + core) * BLOCK, BLOCK), BLOCK)

    def pass_hidden(side, k):
        lanes = lanes_of(side, k)
        return send(at.at[:, lanes], at.at[:, lanes], af_s.at[side, k], af_r.at[side, k], mod=other)

    def relay_hidden(side, k):
        if side or k:
            for s in range(2):
                arrived(at.at[pl.ds(s * SLICE, SLICE), lanes_of(side, k)], a_r.at[side, k, s])
        pass_hidden(side, k).start()

    hid_copy.wait_recv()
    loads[0].wait()
    made = dot(hidf[...], wkv_v[...]).astype(BF)
    for i in range(2):
        for g in range(2):
            kvs[i, g] = made[:, (i * 2 + g) * HS:(i * 2 + g + 1) * HS]
    copy = send(kvs.at[:, other], kvr, pair_s.at[2], pair_r.at[2], mod=other)
    copy.start()
    sent.append(copy)
    def other_kinds():
        for k in range(1, 8):
            for c in range(2):
                arrived(mods.at[(dp - k + 8) % 8 * 2 + (other if c else core)], mod_r.at[k, c])
    arrived(mods.at[dp * 2 + other], mod_r.at[0, 1])
    mine = [
        jnp.broadcast_to(mods[dp * 2 + b][0:1, :], (BLOCK, HS)) == expert for b in range(2)
    ]
    copy.wait_recv()
    for i in range(2):
        for b in range(2):
            rows = slice(b * BLOCK, (b + 1) * BLOCK)
            kvall[i, pl.ds(pl.multiple_of(ctx * CHIP + b * BLOCK, BLOCK), BLOCK), :] = jnp.where(
                mine[b], kvs[i, core, rows, :], kvr[i, rows, :]
            )
    ctx_rows = pl.ds(aligned(ctx, CHIP), CHIP)
    xctx = (1 - xhi) * 4 + z
    xctx_rows = pl.ds(aligned(xctx, CHIP), CHIP)

    def rows_from(side, k):
        return pl.ds(aligned((xhi if side == 0 else 1 - xhi) * 4 + (z - k + 4) % 4, CHIP), CHIP)

    def send_keys(i, side, k, rows, to):
        copy = send(kvall.at[i, rows], kvall.at[i, rows], kv_s.at[i, side, k], kv_r.at[i, side, k], ctx=to)
        copy.start()
        sent.append(copy)

    def keys_from(i, side, k):
        arrived(kvall.at[i, rows_from(side, k)], kv_r.at[i, side, k])

    for i in range(2):
        send_keys(i, 1, 0, ctx_rows, xctx)
    for k in (1, 3, 2):
        for i in range(2):
            send_keys(i, 0, k, ctx_rows, xhi * 4 + (z + k) % 4)

    def project(i):
        group, first, width = q_cols[i]
        loads[1 + i].wait()
        cols = pl.ds(pl.multiple_of(group * GW + first, 128), width)
        qs[group, :, first:first + width] = dot(hidf[...], wq_v[:, cols]).astype(BF)

    project(0)
    for i in range(2):
        keys_from(i, 1, 0)
        for k in (1, 3, 2):
            send_keys(i, 1, k, xctx_rows, xhi * 4 + (z + k) % 4)
    for k in (2, 1, 3):
        send_hidden(1, k)
    project(1)
    q_copy = send(qs.at[other], qr, pair_s.at[3], pair_r.at[3], mod=other)
    q_copy.start()
    sent.append(q_copy)
    project(2)
    project(3)
    seg_rows = segs[:, pl.ds(aligned(ctx, CHIP), CHIP)].astype(F32)
    seg_col = jnp.broadcast_to(seg_rows, (128, CHIP)).T[:, 0:1]
    bias[...] = jnp.where(segs[...].astype(F32) <= seg_col, 0.0, -1e30)
    acc[...] = jnp.zeros_like(acc)
    q_copy.wait_recv()
    for b in range(2):
        rows = slice(b * BLOCK, (b + 1) * BLOCK)
        pick = jnp.broadcast_to(mods[dp * 2 + b][0:1, 0:1], (BLOCK, GW)) == expert
        qf[rows, :] = jnp.where(pick, qs[core, rows, :], qr[rows, :])
    og_copy.wait_recv()
    for i in range(2):
        for k in (1, 3, 2):
            keys_from(i, 0, k)
            keys_from(i, 1, k)

    def one_head(i, carry):
        slot, target = i // 2, i % 2
        head = target * 4 + slot
        lanes = pl.ds(aligned(head, HS), HS)
        full_lanes = pl.ds(aligned(core * HEADS + head, HS), HS)
        q, go = qf[:, lanes], ogf[:, lanes]
        keys, values = kvall[0], kvall[1]
        scores = dot(q, keys, ((1,), (1,))) * (scale * math.log2(math.e)) + bias[...]
        top = jnp.max(scores, axis=1, keepdims=True)
        weights = jnp.exp2(scores - top)
        total = jnp.sum(weights, axis=1, keepdims=True)
        low = weights.astype(BF)
        inv = 1.0 / total
        attended = (dot(low, values) * inv).astype(BF)
        attb[head] = attended
        copy = send(
            attb.at[head, other_rows], attf.at[:, full_lanes], att_s.at[head], att_r.at[head], mod=other
        )
        copy.start()
        attf[:, full_lanes] = attb[head, own_rows, :]
        go32 = go.astype(F32)
        delta = jnp.sum(go32 * attended.astype(F32), axis=1, keepdims=True)
        dprob = dot(go, values, ((1,), (1,)))
        dscore = (weights * (dprob * inv - delta * inv)).astype(BF)
        dq = (dot(dscore, keys) * scale).astype(BF)
        dqb[head] = dq
        gq[:, full_lanes] = dq
        copy = send(dqb.at[head], gq.at[:, full_lanes], gq_s.at[head], gq_r.at[head], mod=other)
        copy.start()
        spread_grads(i, head, target, slot)
        acc[0] += dot(q.T, dscore)
        acc[1] += dot((go32 * inv).astype(BF).T, low)

        @pl.when(i == 2)
        def _():
            for k in (0, 1, 3, 2):
                relay_hidden(0, k)

        @pl.when(i == 4)
        def _():
            for k in (0, 2, 1, 3):
                relay_hidden(1, k)

        return carry

    home = xlo == core

    def cross(head):
        return send(dqb.at[head], dqx.at[head], bx_s.at[head], bx_r.at[head], dp=(1 - xlo) * 4 + y)

    def cross_kv():
        return send(gkv.at[:, core], gkvx, bx_s.at[HEADS], bx_r.at[HEADS], dp=(1 - xlo) * 4 + y)

    def fan(src, side, target, slot, sems, k):
        rows = pl.ds(pl.multiple_of((side * 4 + y) * CHIP, CHIP), CHIP)
        return send(
            src, bg.at[slot, rows], sems.at[k], b_r.at[slot, side * 4 + y], dp=xlo * 4 + (y + k) % 4, mod=target
        )

    def fan_out(src, side, target, slot, sems):
        rows = pl.ds(pl.multiple_of((side * 4 + y) * CHIP, CHIP), CHIP)
        for k in (1, 3, 2):
            fan(src, side, target, slot, sems, k).start()

        @pl.when(target == core)
        def _():
            pltpu.make_async_copy(src, bg.at[slot, rows], b_r.at[slot, side * 4 + y]).start()

        @pl.when(target != core)
        def _():
            fan(src, side, target, slot, sems, 0).start()

    def fan_sent(src, side, target, slot, sems):
        for k in (1, 3, 2):
            fan(src, side, target, slot, sems, k).wait_send()

        @pl.when(target != core)
        def _():
            fan(src, side, target, slot, sems, 0).wait_send()

    def relay_grads(i):
        slot, target = i // 2, i % 2
        head = target * 4 + slot
        arrived(dqx.at[head], bx_r.at[head])
        fan_out(dqx.at[head], 1 - xlo, target, slot, b_s.at[1, head])

    def spread_grads(i, head, target, slot):
        @pl.when(jnp.logical_not(home))
        def _():
            cross(head).start()

        @pl.when(home)
        def _():
            fan_out(dqb.at[head], xlo, target, slot, b_s.at[0, head])

            @pl.when(i >= LAG)
            def _():
                relay_grads(i - LAG)

    def block_sums(slot):
        for source in range(8):
            arrived(bg.at[slot, pl.ds(source * CHIP, CHIP)], b_r.at[slot, source])
        for t in range(16):
            rows = slice(t * BLOCK, (t + 1) * BLOCK)
            kind = mods[t][0:1, :]
            block = bg[slot, rows, :]
            second = jnp.where(jnp.broadcast_to(kind, (BLOCK, HS)) == 1.0, block, jnp.zeros_like(block))
            be[rows, HS:] = second
            be[rows, :HS] = block - second
        cf[...] = dot(at[...], be[...])
        for c in range(8):
            for e, buf in enumerate((cs, cs1)):
                cols = slice(e * HS, (e + 1) * HS)
                both = jnp.concatenate(
                    [cf[c * PART:(c + 1) * PART, cols], cf[SLICE + c * PART:SLICE + (c + 1) * PART, cols]], axis=0
                )
                buf[slot, c % 4, c // 4] = both.astype(BF)

    def z_leg(slot, k):
        to = (z + k) % 4
        return send(cs.at[slot, to], crz.at[slot, k - 1], c_s.at[slot, k], c_r.at[slot, k], ctx=xhi * 4 + to)

    def x_leg(slot):
        return send(cs1.at[slot, :, 1 - xhi], crx.at[slot], c_s.at[slot, 0], c_r.at[slot, 0], ctx=xctx)

    def then_x(slot):
        return send(cx.at[slot], cxr.at[slot], cx_s.at[slot, 0], cx_r.at[slot, 0], ctx=xctx)

    def then_z(slot, k):
        to = (z + k) % 4
        return send(cz.at[slot, to], czr.at[slot, k - 1], cx_s.at[slot, k], cx_r.at[slot, k], ctx=xhi * 4 + to)

    def z_legs(slot):
        for k in (1, 3, 2):
            z_leg(slot, k).start()

    def x_legs(slot):
        x_leg(slot).start()

    def first_leg(slot):
        x_legs(slot)
        z_legs(slot)

    def second_leg(slot):
        arrived(crx.at[slot], c_r.at[slot, 0])
        for k in (1, 3, 2):
            to = (z + k) % 4
            cz[slot, to] = (cs1[slot, to, xhi].astype(F32) + crx[slot, to].astype(F32)).astype(BF)
            then_z(slot, k).start()
        keep[slot, 1] = cs1[slot, z, xhi].astype(F32) + crx[slot, z].astype(F32)
        for k in (1, 3, 2):
            arrived(crz.at[slot, k - 1], c_r.at[slot, k])
        total = cs[slot, z, 1 - xhi].astype(F32)
        for k in range(3):
            total += crz[slot, k, 1 - xhi].astype(F32)
        cx[slot] = total.astype(BF)
        then_x(slot).start()
        total = cs[slot, z, xhi].astype(F32)
        for k in range(3):
            total += crz[slot, k, xhi].astype(F32)
        keep[slot, 0] = total

    def last_leg(slot):
        for k in (1, 3, 2):
            arrived(czr.at[slot, k - 1], cx_r.at[slot, k])
        arrived(cxr.at[slot], cx_r.at[slot, 0])
        second = keep[slot, 1]
        for k in range(3):
            second += czr[slot, k].astype(F32)
        for e, total in enumerate((keep[slot, 0] + cxr[slot].astype(F32), second)):
            for s in range(2):
                padded = jnp.concatenate([total[s * PART:(s + 1) * PART], jnp.zeros((8, HS), F32)], axis=0)
                fin[s, e, slot] = padded.astype(BF)

    def each(step):
        def run(slot, carry):
            step(slot)
            return carry

        return run

    lax.fori_loop(0, HEADS, one_head, 0)

    @pl.when(home)
    def _():
        for i in range(HEADS - LAG, HEADS):
            relay_grads(i)

    for c in range(8):
        for i in range(2):
            dkvb[i, c // 4, c % 4] = acc[i, :, c * CHIP:(c + 1) * CHIP].astype(BF)
    copies = [send(dkvb.at[1, 1 - xhi], dvr, dk_s.at[0], dk_r.at[0], ctx=xctx)]
    for k in (1, 3, 2):
        to = (z + k) % 4
        copies.append(send(dkvb.at[0, :, to], dkr.at[k - 1], dk_s.at[k], dk_r.at[k], ctx=xhi * 4 + to))
    for copy in copies:
        copy.start()
        sent.append(copy)

    last = 5 - core
    for side in range(2):
        for k in range(4):
            lanes = pl.ds(
                pl.multiple_of((((xlo if side == 0 else 1 - xlo) * 4 + (y - k + 4) % 4) * 2 + other) * BLOCK, BLOCK),
                BLOCK,
            )
            arrived(at.at[:, lanes], af_r.at[side, k])
    other_kinds()
    lax.fori_loop(0, 2, each(block_sums), 0)
    for head in range(HEADS):
        arrived(gq.at[:, pl.ds(aligned(other * HEADS + head, HS), HS)], gq_r.at[head])

    def spread(i, carry):
        rows = pl.ds(aligned(i, 512), 512)
        total = dot(gq[...], wq_v[rows, :], ((1,), (1,)))
        high = total.astype(BF)
        hidf[:, rows] = high
        sb[:, rows] = (total - high.astype(F32)).astype(BF)
        return carry

    lax.fori_loop(0, 7, spread, 0)

    copies[0].wait_recv()
    for k in (1, 3, 2):
        to = (z + k) % 4
        lanes = pl.ds(pl.multiple_of((xhi * 4 + to) * CHIP, CHIP), CHIP)
        dvz[to] = (acc[1, :, lanes] + dvr[to].astype(F32)).astype(BF)
        copy = send(dvz.at[to], dvzr.at[k - 1], dk_s.at[4 + k], dk_r.at[4 + k], ctx=xhi * 4 + to)
        copy.start()
        sent.append(copy)
    for k in (1, 3, 2):
        arrived(dkr.at[k - 1], dk_r.at[k])

    def over_z(half):
        total = acc[0, :, pl.ds(pl.multiple_of((half * 4 + z) * CHIP, CHIP), CHIP)]
        for k in range(3):
            total += dkr[k, half].astype(F32)
        return total

    dkx[...] = over_z(1 - xhi).astype(BF)
    dk_copy = send(dkx, dkxr, dk_s.at[4], dk_r.at[4], ctx=xctx)
    dk_copy.start()
    sent.append(dk_copy)
    lax.fori_loop(0, 2, each(first_leg), 0)
    lax.fori_loop(2, last - 1, each(block_sums), 0)
    dk = over_z(xhi)
    dv = acc[1, :, pl.ds(pl.multiple_of((xhi * 4 + z) * CHIP, CHIP), CHIP)] + dvr[z].astype(F32)
    for k in (1, 3, 2):
        arrived(dvzr.at[k - 1], dk_r.at[4 + k])
    for k in range(3):
        dv += dvzr[k].astype(F32)
    gkv[1, core] = dv.T.astype(BF)
    dk_copy.wait_recv()
    dk = (dk + dkxr[...].astype(F32)) * scale
    gkv[0, core] = dk.T.astype(BF)
    gkv_copy = send(gkv.at[:, core], gkv.at[:, core], pair_s.at[4], pair_r.at[4], mod=other)
    gkv_copy.start()
    sent.append(gkv_copy)

    @pl.when(jnp.logical_not(home))
    def _():
        cross_kv().start()

    @pl.when(home)
    def _():
        for i, target, slot in ((0, 0, 4), (1, 1, 3)):
            fan_out(gkv.at[i, core], xlo, target, slot, b_s.at[0, HEADS + i])

    lax.fori_loop(2, last - 1, each(first_leg), 0)
    lax.fori_loop(0, 2, each(second_leg), 0)

    @pl.when(home)
    def _():
        arrived(gkvx, bx_r.at[HEADS])
        for i, target, slot in ((0, 0, 4), (1, 1, 3)):
            fan_out(gkvx.at[i], 1 - xlo, target, slot, b_s.at[1, HEADS + i])

    arrived(gkv.at[:, other], pair_r.at[4])
    grads_kv = jnp.concatenate([gkv[0, 0], gkv[0, 1], gkv[1, 0], gkv[1, 1]], axis=1)
    for i in range(7):
        rows = slice(i * 512, (i + 1) * 512)
        total = hidf[:, rows].astype(F32) + sb[:, rows].astype(F32) + dot(grads_kv, wkv_v[rows, :], ((1,), (1,)))
        sb[:, rows] = total.astype(BF)
    home_copy = send(sb.at[other_rows], sr, pair_s.at[5], pair_r.at[5], mod=other)
    home_copy.start()
    sent.append(home_copy)

    block_sums(last - 1)
    first_leg(last - 1)

    fin[...] = jnp.zeros_like(fin)
    lax.fori_loop(2, last, each(second_leg), 0)
    lax.fori_loop(0, last, each(last_leg), 0)
    for s in range(2):
        for e in range(2):
            at_home = jnp.logical_and(xlo == s, core == e)
            copy = send(
                fin.at[s, e], finr.at[xlo, core], fin_s.at[s, e], fin_r.at[xlo, core], dp=s * 4 + y, mod=e
            )

            @pl.when(at_home)
            def _():
                pltpu.make_async_copy(fin.at[s, e], finr.at[xlo, core], fin_r.at[xlo, core]).start()

            @pl.when(jnp.logical_not(at_home))
            def _():
                copy.start()

    for head in range(HEADS):
        lanes = pl.ds(aligned(other * HEADS + head, HS), HS)
        arrived(attf.at[:, lanes], att_r.at[head])
    arrived(sr, pair_r.at[5])
    pick = jnp.broadcast_to(mods[here][0:1, 0:1], (BLOCK, D)) == expert
    gh_o[...] = jnp.where(pick, sb[own_rows, :], sr[...])

    for g in range(2):
        for c in range(2):
            arrived(finr.at[g, c], fin_r.at[g, c])

    for copy in sent:
        copy.wait_send()

    def heads_sent(head, carry):
        full_lanes = pl.ds(aligned(core * HEADS + head, HS), HS)
        send(
            attb.at[head, other_rows], attf.at[:, full_lanes], att_s.at[head], att_r.at[head], mod=other
        ).wait_send()
        send(dqb.at[head], gq.at[:, full_lanes], gq_s.at[head], gq_r.at[head], mod=other).wait_send()

        @pl.when(jnp.logical_not(home))
        def _():
            cross(head).wait_send()

        @pl.when(home)
        def _():
            fan_sent(dqb.at[head], xlo, head // 4, head % 4, b_s.at[0, head])
            fan_sent(dqx.at[head], 1 - xlo, head // 4, head % 4, b_s.at[1, head])

        return carry

    lax.fori_loop(0, HEADS, heads_sent, 0)
    for side in range(2):
        for k in range(4):
            pass_hidden(side, k).wait_send()

    @pl.when(jnp.logical_not(home))
    def _():
        cross_kv().wait_send()

    @pl.when(home)
    def _():
        for i, target, slot in ((0, 0, 4), (1, 1, 3)):
            fan_sent(gkv.at[i, core], xlo, target, slot, b_s.at[0, HEADS + i])
            fan_sent(gkvx.at[i], 1 - xlo, target, slot, b_s.at[1, HEADS + i])

    def blocks_sent(slot, carry):
        x_leg(slot).wait_send()
        then_x(slot).wait_send()
        for k in (1, 3, 2):
            z_leg(slot, k).wait_send()
            then_z(slot, k).wait_send()
        return carry

    lax.fori_loop(0, last, blocks_sent, 0)
    for s in range(2):
        for e in range(2):
            copy = send(
                fin.at[s, e], finr.at[xlo, core], fin_s.at[s, e], fin_r.at[xlo, core], dp=s * 4 + y, mod=e
            )

            @pl.when(jnp.logical_not(jnp.logical_and(xlo == s, core == e)))
            def _():
                copy.wait_send()


def results(att, gh, fin, att_o, gh_o, gwq_o, gwkv_o):
    att_o[...] = att[...]
    gh_o[...] = gh[...]
    for g in range(2):
        for head in range(HEADS):
            cols = slice((g * HEADS + head) * HS, (g * HEADS + head + 1) * HS)
            gwq_o[:, cols] = fin[g, head // 4, head % 4][:PART]
        gwkv_o[:, g * HS:(g + 1) * HS] = fin[g, 0, 4][:PART]
        gwkv_o[:, KW + g * HS:KW + (g + 1) * HS] = fin[g, 1, 3][:PART]


def on_device(hidden_in, out_grad, modality, segment, w_query, w_keyval):
    vmem, dma = pltpu.VMEM, pltpu.SemaphoreType.DMA
    scratch = [
        vmem((BLOCK, D), BF), vmem((BLOCK, QW), BF), vmem((D, QW), BF), vmem((D, 2 * KW), BF),
        vmem((CHIP, D), BF), vmem((D, BLOCK), BF), vmem((CHIP, GW), BF), vmem((16, 8, HS), F32),
        vmem((2 * SLICE, SEQ), BF),
        vmem((2, 2, CHIP, HS), BF), vmem((2, CHIP, HS), BF), vmem((2, SEQ, HS), BF),
        vmem((2, CHIP, GW), BF), vmem((CHIP, GW), BF), vmem((CHIP, GW), BF), vmem((CHIP, SEQ), F32),
        vmem((8, BLOCK), F32), vmem((HEADS, CHIP, HS), BF), vmem((HEADS, CHIP, HS), BF), vmem((HEADS, CHIP, HS), BF), vmem((CHIP, QW), BF),
        vmem((2, HS, SEQ), F32), vmem((2, 2, 4, HS, CHIP), BF), vmem((3, 2, HS, CHIP), BF), vmem((4, HS, CHIP), BF), vmem((4, HS, CHIP), BF), vmem((3, HS, CHIP), BF),
        vmem((HS, CHIP), BF), vmem((HS, CHIP), BF), vmem((2, 2, CHIP, HS), BF), vmem((2, CHIP, HS), BF),
        vmem((5, SEQ, HS), BF), vmem((SEQ, 2 * HS), BF), vmem((2 * SLICE, 2 * HS), F32),
        vmem((5, 4, 2, 2 * PART, HS), BF), vmem((5, 4, 2, 2 * PART, HS), BF), vmem((5, 3, 2, 2 * PART, HS), BF), vmem((5, 4, 2 * PART, HS), BF),
        vmem((5, 2 * PART, HS), BF), vmem((5, 2 * PART, HS), BF), vmem((5, 4, 2 * PART, HS), BF), vmem((5, 3, 2 * PART, HS), BF), vmem((5, 2, 2 * PART, HS), F32),
        vmem((2, 2, 5, 64, HS), BF),
        vmem((CHIP, D), BF), vmem((BLOCK, D), BF),
        dma((7,)), dma((6,)), dma((6,)), dma((8, 2)), dma((8, 2)), dma((2, 4, 2)), dma((2, 4, 2)), dma((2, 4)), dma((2, 4)),
        dma((2, 2, 4)), dma((2, 2, 4)), dma((HEADS,)), dma((HEADS,)), dma((HEADS,)), dma((HEADS,)),
        dma((HEADS + 1,)), dma((HEADS + 1,)), dma((2, 9, 4)), dma((5, 8)), dma((8,)), dma((8,)), dma((5, 4)), dma((5, 4)), dma((5, 4)), dma((5, 4)),
        dma((2, 2)), dma((2, 2)),
    ]
    in_vmem, anywhere = pl.BlockSpec(memory_space=pltpu.VMEM), pl.BlockSpec(memory_space=pl.ANY)
    raw = pl.pallas_call(
        layer,
        out_shape=(
            jax.ShapeDtypeStruct((BLOCK, QW), BF),
            jax.ShapeDtypeStruct((BLOCK, D), BF),
            jax.ShapeDtypeStruct((2, 2, 5, 64, HS), BF),
        ),
        in_specs=[anywhere] * 2 + [in_vmem] * 2 + [anywhere] * 2,
        out_specs=(in_vmem,) * 3,
        scratch_shapes=scratch,
        compiler_params=pltpu.CompilerParams(
            collective_id=0, has_side_effects=True, vmem_limit_bytes=63 * 2**20
        ),
        name="layer",
    )(hidden_in[0], out_grad[0], modality, segment, w_query[0], w_keyval[0])
    attended, grad_hidden, grad_wq, grad_wkv = pl.pallas_call(
        results,
        out_shape=(
            jax.ShapeDtypeStruct((BLOCK, QW), BF),
            jax.ShapeDtypeStruct((BLOCK, D), BF),
            jax.ShapeDtypeStruct((PART, QW), BF),
            jax.ShapeDtypeStruct((PART, 2 * KW), BF),
        ),
        in_specs=[in_vmem] * 3,
        out_specs=(in_vmem,) * 4,
        name="results",
    )(*raw)
    return attended[None], grad_hidden[None], grad_wq[None], grad_wkv[None]


def solution(mesh):
    return jax.shard_map(
        on_device,
        mesh=mesh,
        in_specs=(
            P("dp", ("ctx", "mod"), None),
            P("dp", ("ctx", "mod"), None),
            P("dp", ("ctx", "mod")),
            P("dp", None),
            P("mod", None, None),
            P("mod", None, None),
        ),
        out_specs=(
            P("dp", ("ctx", "mod"), None),
            P("dp", ("ctx", "mod"), None),
            P("mod", ("dp", "ctx"), None),
            P("mod", ("dp", "ctx"), None),
        ),
        check_vma=False,
    )
```

```python
import functools
import math

import jax
import jax.numpy as jnp
from jax import lax
from jax.experimental import pallas as pl
from jax.experimental.pallas import tpu as pltpu
from jax.sharding import PartitionSpec as P

HS = 128
BLOCK = 128
D = 3584
QW = 1792
KW = 256
SEQ = 2048
HEADS = 7
GW = HEADS * HS
CHIP = 2 * BLOCK
SLICE = 448
PART = 56
MESH = pl.DeviceIdType.MESH
BF = jnp.bfloat16
F32 = jnp.float32


def aligned(index, step):
    return pl.multiple_of(index * step, step)


def dot(a, b, dims=((1,), (0,))):
    return lax.dot_general(a, b, (dims, ((), ())), preferred_element_type=F32)


def send(src, dst, send_sem, recv_sem, **device):
    return pltpu.make_async_remote_copy(
        src_ref=src, dst_ref=dst, send_sem=send_sem, recv_sem=recv_sem,
        device_id=device, device_id_type=MESH,
    )


def arrived(dst, sem):
    pltpu.make_async_copy(dst, dst, sem).wait()


def layer(
    hid_h, og_h, kinds_h, segs_h, wq, wkv,
    att_o, gh_o, finr,
    hid, og, kinds, segs, attf, ghf, wq_v, wkv_v, hidf, hid_t, ogf, mods, at, kvs, kvr, kvall, qs, qr, qf, bias,
    modv, attb, dqb, dqx, gq, acc, dkvb, dkr, dvr, dvz, dvzr, dkx, dkxr, gkv, bg, be, cf, cs, cs1, crz, crz1, crx, cx, cxr, cz, czr, keep, fin, sb, sr,
    w_sem, pair_s, pair_r, mod_s, mod_r, a_s, a_r, af_s, af_r, kv_s, kv_r,
    att_s, att_r, gq_s, gq_r, bx_s, bx_r, b_s, b_r, dk_s, dk_r, c_s, c_r, cx_s, cx_r, fin_s, fin_r,
):
    dp, ctx, core = lax.axis_index("dp"), lax.axis_index("ctx"), lax.axis_index("mod")
    xlo, y, xhi, z = dp // 4, dp % 4, ctx // 4, ctx % 4
    other = 1 - core
    here = dp * 2 + core
    expert = core.astype(F32)
    scale = 1.0 / math.sqrt(HS)

    q_cols = []
    for group in (other, core):
        for first, width in ((0, 512), (512, 384)):
            q_cols.append((group, first, width))
    own_loads = [
        pltpu.make_async_copy(hid_h, hid, w_sem.at[5]), pltpu.make_async_copy(og_h, og, w_sem.at[6]),
        pltpu.make_async_copy(kinds_h, kinds, w_sem.at[9]), pltpu.make_async_copy(segs_h, segs, w_sem.at[10]),
    ]
    loads = [pltpu.make_async_copy(wkv, wkv_v, w_sem.at[0])]
    for i, (group, first, width) in enumerate(q_cols):
        cols = pl.ds(pl.multiple_of(group * GW + first, 128), width)
        loads.append(pltpu.make_async_copy(wq.at[:, cols], wq_v.at[:, cols], w_sem.at[1 + i]))
    barrier = pltpu.get_barrier_semaphore()
    for k in range(8):
        pl.semaphore_signal(barrier, inc=1, device_id={"dp": (dp + k) % 8, "mod": other}, device_id_type=MESH)
        if k:
            pl.semaphore_signal(barrier, inc=1, device_id={"dp": (dp + k) % 8}, device_id_type=MESH)
            pl.semaphore_signal(barrier, inc=1, device_id={"ctx": (ctx + k) % 8}, device_id_type=MESH)
    for load in own_loads + loads:
        load.start()
    for load in own_loads:
        load.wait()
    pl.semaphore_wait(barrier, 22)

    own_rows = pl.ds(aligned(core, BLOCK), BLOCK)
    other_rows = pl.ds(aligned(other, BLOCK), BLOCK)
    sent = []

    hid_copy = send(hid, hidf.at[own_rows], pair_s.at[0], pair_r.at[0], mod=other)
    hid_copy.start()
    og_copy = send(og.at[:, pl.ds(aligned(other, GW), GW)], ogf.at[own_rows], pair_s.at[1], pair_r.at[1], mod=other)
    og_copy.start()
    sent += [hid_copy, og_copy]
    modv[...] = jnp.broadcast_to(kinds[...].astype(F32), (8, BLOCK))
    mods[here] = modv[...]
    for k in range(8):
        for c in range(2):
            if k == 0 and c == 0:
                continue
            dev = {"dp": (dp + k) % 8, "mod": other if c else core}
            copy = send(modv, mods.at[here], mod_s.at[k, c], mod_r.at[k, c], **dev)
            copy.start()
            sent.append(copy)
    hidf[own_rows, :] = hid[...]
    ogf[own_rows, :] = og[:, pl.ds(aligned(core, GW), GW)]

    here_lanes = pl.ds(aligned(here, BLOCK), BLOCK)
    for i in range(7):
        hid_t[i * 512:(i + 1) * 512, :] = hid[:, i * 512:(i + 1) * 512].T
    def hidden_copy(side, k, s):
        to = (y + k) % 4
        rows = pl.ds(pl.multiple_of((s * 4 + to) * SLICE, 64), SLICE)
        return send(
            hid_t.at[rows], at.at[pl.ds(s * SLICE, SLICE), here_lanes], a_s.at[side, k, s], a_r.at[side, k, s],
            dp=(xlo if side == 0 else 1 - xlo) * 4 + to,
        )

    def send_hidden(side, k):
        for s in range(2):
            hidden_copy(side, k, s).start()

    for side, k in ((1, 0), (0, 1), (0, 3), (0, 2)):
        send_hidden(side, k)
    for s in range(2):
        rows = pl.ds(pl.multiple_of((s * 4 + y) * SLICE, 64), SLICE)
        at[s * SLICE:(s + 1) * SLICE, here_lanes] = hid_t[rows, :]

    def lanes_of(side, k):
        return pl.ds(pl.multiple_of((((xlo if side == 0 else 1 - xlo) * 4 + (y - k + 4) % 4) * 2 + core) * BLOCK, BLOCK), BLOCK)

    def pass_hidden(side, k):
        lanes = lanes_of(side, k)
        return send(at.at[:, lanes], at.at[:, lanes], af_s.at[side, k], af_r.at[side, k], mod=other)

    def relay_hidden(side, k):
        if side or k:
            for s in range(2):
                arrived(at.at[pl.ds(s * SLICE, SLICE), lanes_of(side, k)], a_r.at[side, k, s])
        pass_hidden(side, k).start()

    loads[0].wait()

    def key_rows(rows):
        made = dot(hidf[rows, :], wkv_v[...]).astype(BF)
        for i in range(2):
            for g in range(2):
                kvs[i, g, rows, :] = made[:, (i * 2 + g) * HS:(i * 2 + g + 1) * HS]

    key_rows(own_rows)
    hid_copy.wait_recv()
    key_rows(other_rows)
    copy = send(kvs.at[:, other], kvr, pair_s.at[2], pair_r.at[2], mod=other)
    copy.start()
    sent.append(copy)
    def other_kinds():
        for k in range(1, 8):
            for c in range(2):
                arrived(mods.at[(dp - k + 8) % 8 * 2 + (other if c else core)], mod_r.at[k, c])
    arrived(mods.at[dp * 2 + other], mod_r.at[0, 1])
    mine = [
        jnp.broadcast_to(mods[dp * 2 + b][0:1, :], (BLOCK, HS)) == expert for b in range(2)
    ]
    copy.wait_recv()
    for i in range(2):
        for b in range(2):
            rows = slice(b * BLOCK, (b + 1) * BLOCK)
            kvall[i, pl.ds(pl.multiple_of(ctx * CHIP + b * BLOCK, BLOCK), BLOCK), :] = jnp.where(
                mine[b], kvs[i, core, rows, :], kvr[i, rows, :]
            )
    ctx_rows = pl.ds(aligned(ctx, CHIP), CHIP)
    xctx = (1 - xhi) * 4 + z
    xctx_rows = pl.ds(aligned(xctx, CHIP), CHIP)

    def rows_from(side, k):
        return pl.ds(aligned((xhi if side == 0 else 1 - xhi) * 4 + (z - k + 4) % 4, CHIP), CHIP)

    def send_keys(i, side, k, rows, to):
        copy = send(kvall.at[i, rows], kvall.at[i, rows], kv_s.at[i, side, k], kv_r.at[i, side, k], ctx=to)
        copy.start()
        sent.append(copy)

    def keys_from(i, side, k):
        arrived(kvall.at[i, rows_from(side, k)], kv_r.at[i, side, k])

    for i in range(2):
        send_keys(i, 1, 0, ctx_rows, xctx)
    for k in (1, 3, 2):
        for i in range(2):
            send_keys(i, 0, k, ctx_rows, xhi * 4 + (z + k) % 4)

    def project(i):
        group, first, width = q_cols[i]
        loads[1 + i].wait()
        cols = pl.ds(pl.multiple_of(group * GW + first, 128), width)
        qs[group, :, first:first + width] = dot(hidf[...], wq_v[:, cols]).astype(BF)

    project(0)
    for i in range(2):
        keys_from(i, 1, 0)
        for k in (1, 3, 2):
            send_keys(i, 1, k, xctx_rows, xhi * 4 + (z + k) % 4)
    for k in (2, 1, 3):
        send_hidden(1, k)
    project(1)
    q_copy = send(qs.at[other], qr, pair_s.at[3], pair_r.at[3], mod=other)
    q_copy.start()
    sent.append(q_copy)
    project(2)
    project(3)
    seg_rows = segs[:, pl.ds(aligned(ctx, CHIP), CHIP)].astype(F32)
    seg_col = jnp.broadcast_to(seg_rows, (128, CHIP)).T[:, 0:1]
    bias[...] = jnp.where(segs[...].astype(F32) <= seg_col, 0.0, -1e30)
    acc[...] = jnp.zeros_like(acc)
    q_copy.wait_recv()
    for b in range(2):
        rows = slice(b * BLOCK, (b + 1) * BLOCK)
        pick = jnp.broadcast_to(mods[dp * 2 + b][0:1, 0:1], (BLOCK, GW)) == expert
        qf[rows, :] = jnp.where(pick, qs[core, rows, :], qr[rows, :])
    og_copy.wait_recv()
    for i in range(2):
        for k in (1, 3, 2):
            keys_from(i, 0, k)
            keys_from(i, 1, k)

    last = 5 - core

    def head_scores(head):
        q = qf[:, pl.ds(aligned(head, HS), HS)]
        return dot(q, kvall[0], ((1,), (1,))) * (scale * math.log2(math.e)) + bias[...]

    def rest_of_head(head, scores):
        lanes = pl.ds(aligned(head, HS), HS)
        full_lanes = pl.ds(aligned(core * HEADS + head, HS), HS)
        q, go = qf[:, lanes], ogf[:, lanes]
        keys, values = kvall[0], kvall[1]
        top = jnp.max(scores, axis=1, keepdims=True)
        weights = jnp.exp2(scores - top)
        total = jnp.sum(weights, axis=1, keepdims=True)
        low = weights.astype(BF)
        inv = 1.0 / total
        attended = (dot(low, values) * inv).astype(BF)
        attb[head] = attended
        copy = send(
            attb.at[head, other_rows], attf.at[:, full_lanes], att_s.at[head], att_r.at[head], mod=other
        )
        copy.start()
        attf[:, full_lanes] = attb[head, own_rows, :]
        go32 = go.astype(F32)
        delta = jnp.sum(go32 * attended.astype(F32), axis=1, keepdims=True)
        dprob = dot(go, values, ((1,), (1,)))
        dscore = (weights * (dprob * inv - delta * inv)).astype(BF)
        dq = (dot(dscore, keys) * scale).astype(BF)
        dqb[head] = dq
        gq[:, full_lanes] = dq
        copy = send(dqb.at[head], gq.at[:, full_lanes], gq_s.at[head], gq_r.at[head], mod=other)
        copy.start()
        acc[0] += dot(q.T, dscore)
        acc[1] += dot((go32 * inv).astype(BF).T, low)

    def two_heads(p, carry):
        first, second = head_scores(p), head_scores(4 + p)
        rest_of_head(p, first)
        rest_of_head(4 + p, second)
        spread_grads(p, 0, p)
        spread_grads(4 + p, 1, p)

        @pl.when(jnp.logical_and(home, p == 2))
        def _():
            relay_grads(0)
            relay_grads(1)

        @pl.when(p == 1)
        def _():
            for k in range(4):
                relay_hidden(0, k)

        @pl.when(p == 2)
        def _():
            for k in (0, 2, 1, 3):
                relay_hidden(1, k)

        return carry

    home = xlo == core

    def cross(head):
        return send(dqb.at[head], dqx.at[head], bx_s.at[head], bx_r.at[head], dp=(1 - xlo) * 4 + y)

    def straight(src, target, slot, sems, k):
        rows = pl.ds(aligned(dp, CHIP), CHIP)
        return send(
            src, bg.at[slot, rows], sems.at[k], b_r.at[slot, dp], dp=core * 4 + (y + k) % 4, mod=target
        )

    def straight_out(src, target, slot, sems):
        at_home = jnp.logical_and(home, target == core)
        rows = pl.ds(aligned(dp, CHIP), CHIP)
        for k in (1, 3, 2):
            straight(src, target, slot, sems, k).start()

        @pl.when(at_home)
        def _():
            pltpu.make_async_copy(src, bg.at[slot, rows], b_r.at[slot, dp]).start()

        @pl.when(jnp.logical_not(at_home))
        def _():
            straight(src, target, slot, sems, 0).start()

    def straight_sent(src, target, slot, sems):
        for k in (1, 3, 2):
            straight(src, target, slot, sems, k).wait_send()

        @pl.when(jnp.logical_not(jnp.logical_and(home, target == core)))
        def _():
            straight(src, target, slot, sems, 0).wait_send()

    def fan(src, side, target, slot, sems, k):
        rows = pl.ds(pl.multiple_of((side * 4 + y) * CHIP, CHIP), CHIP)
        return send(
            src, bg.at[slot, rows], sems.at[k], b_r.at[slot, side * 4 + y], dp=xlo * 4 + (y + k) % 4, mod=target
        )

    def fan_out(src, side, target, slot, sems):
        rows = pl.ds(pl.multiple_of((side * 4 + y) * CHIP, CHIP), CHIP)
        for k in (1, 3, 2):
            fan(src, side, target, slot, sems, k).start()

        @pl.when(target == core)
        def _():
            pltpu.make_async_copy(src, bg.at[slot, rows], b_r.at[slot, side * 4 + y]).start()

        @pl.when(target != core)
        def _():
            fan(src, side, target, slot, sems, 0).start()

    def fan_sent(src, side, target, slot, sems):
        for k in (1, 3, 2):
            fan(src, side, target, slot, sems, k).wait_send()

        @pl.when(target != core)
        def _():
            fan(src, side, target, slot, sems, 0).wait_send()

    def relay_grads(i):
        slot, target = i // 2, i % 2
        head = target * 4 + slot
        arrived(dqx.at[head], bx_r.at[head])
        fan_out(dqx.at[head], 1 - xlo, target, slot, b_s.at[1, head])

    def spread_grads(head, target, slot):
        @pl.when(jnp.logical_not(home))
        def _():
            cross(head).start()

        @pl.when(home)
        def _():
            fan_out(dqb.at[head], xlo, target, slot, b_s.at[0, head])

    def block_sums(slot):
        for source in range(8):
            arrived(bg.at[slot, pl.ds(source * CHIP, CHIP)], b_r.at[slot, source])
        for t in range(16):
            rows = slice(t * BLOCK, (t + 1) * BLOCK)
            kind = mods[t][0:1, :]
            block = bg[slot, rows, :]
            second = jnp.where(jnp.broadcast_to(kind, (BLOCK, HS)) == 1.0, block, jnp.zeros_like(block))
            be[rows, HS:] = second
            be[rows, :HS] = block - second
        cf[...] = dot(at[...], be[...])
        for c in range(8):
            for e, buf in enumerate((cs, cs1)):
                cols = slice(e * HS, (e + 1) * HS)
                both = jnp.concatenate(
                    [cf[c * PART:(c + 1) * PART, cols], cf[SLICE + c * PART:SLICE + (c + 1) * PART, cols]], axis=0
                )
                buf[slot, c % 4, c // 4] = both.astype(BF)

    def z_leg(slot, k):
        to = (z + k) % 4
        return send(cs.at[slot, to], crz.at[slot, k - 1], c_s.at[slot, k], c_r.at[slot, k], ctx=xhi * 4 + to)

    def z_leg1(slot, k):
        to = (z + k) % 4
        return send(cs1.at[slot, to], crz1.at[slot, k - 1], c_s.at[slot, 3 + k], c_r.at[slot, 3 + k], ctx=xhi * 4 + to)

    def x_leg():
        return send(cs1.at[last - 1, :, 1 - xhi], crx, c_s.at[last - 1, 0], c_r.at[last - 1, 0], ctx=xctx)

    def then_x(slot):
        return send(cx.at[slot, 0], cxr.at[slot, 0], cx_s.at[slot, 0], cx_r.at[slot, 0], ctx=xctx)

    def then_x1(slot):
        return send(cx.at[slot, 1], cxr.at[slot, 1], cx_s.at[slot, 1], cx_r.at[slot, 1], ctx=xctx)

    def then_z(k):
        to = (z + k) % 4
        return send(cz.at[to], czr.at[k - 1], cx_s.at[5, k], cx_r.at[5, k], ctx=xhi * 4 + to)

    def first_leg(slot):
        for k in (1, 3, 2):
            z_leg(slot, k).start()
            z_leg1(slot, k).start()

    def last_first_leg():
        x_leg().start()
        for k in (1, 3, 2):
            z_leg(last - 1, k).start()

    def over_z_sums(mine, came, slot, half):
        total = mine[slot, z, half].astype(F32)
        for k in range(3):
            total += came[slot, k, half].astype(F32)
        return total

    def second_leg(slot):
        for k in (1, 3, 2):
            arrived(crz.at[slot, k - 1], c_r.at[slot, k])
            arrived(crz1.at[slot, k - 1], c_r.at[slot, 3 + k])
        cx[slot, 0] = over_z_sums(cs, crz, slot, 1 - xhi).astype(BF)
        then_x(slot).start()
        cx[slot, 1] = over_z_sums(cs1, crz1, slot, 1 - xhi).astype(BF)
        then_x1(slot).start()
        keep[slot, 0] = over_z_sums(cs, crz, slot, xhi)
        keep[slot, 1] = over_z_sums(cs1, crz1, slot, xhi)

    def last_second_leg():
        slot = last - 1
        for k in (1, 3, 2):
            arrived(crz.at[slot, k - 1], c_r.at[slot, k])
        cx[slot, 0] = over_z_sums(cs, crz, slot, 1 - xhi).astype(BF)
        then_x(slot).start()
        arrived(crx, c_r.at[slot, 0])
        for k in (1, 3, 2):
            to = (z + k) % 4
            cz[to] = (cs1[slot, to, xhi].astype(F32) + crx[to].astype(F32)).astype(BF)
            then_z(k).start()
        keep[slot, 0] = over_z_sums(cs, crz, slot, xhi)
        keep[slot, 1] = cs1[slot, z, xhi].astype(F32) + crx[z].astype(F32)

    def finish(slot, totals):
        for e, total in enumerate(totals):
            for s in range(2):
                padded = jnp.concatenate([total[s * PART:(s + 1) * PART], jnp.zeros((8, HS), F32)], axis=0)
                fin[slot, s, e] = padded.astype(BF)

    def last_leg(slot):
        arrived(cxr.at[slot, 0], cx_r.at[slot, 0])
        arrived(cxr.at[slot, 1], cx_r.at[slot, 1])
        finish(slot, [keep[slot, e] + cxr[slot, e].astype(F32) for e in range(2)])

    def last_last_leg():
        slot = last - 1
        arrived(cxr.at[slot, 0], cx_r.at[slot, 0])
        second = keep[slot, 1]
        for k in (1, 3, 2):
            arrived(czr.at[k - 1], cx_r.at[5, k])
            second += czr[k - 1].astype(F32)
        finish(slot, [keep[slot, 0] + cxr[slot, 0].astype(F32), second])

    def each(step):
        def run(slot, carry):
            step(slot)
            return carry

        return run

    lax.fori_loop(0, 3, two_heads, 0)
    rest_of_head(3, head_scores(3))
    spread_grads(3, 0, 3)

    for c in range(8):
        for i in range(2):
            dkvb[i, c // 4, c % 4] = acc[i, :, c * CHIP:(c + 1) * CHIP].astype(BF)
    copies = [send(dkvb.at[1, 1 - xhi], dvr, dk_s.at[0], dk_r.at[0], ctx=xctx)]
    for k in (1, 3, 2):
        to = (z + k) % 4
        copies.append(send(dkvb.at[0, :, to], dkr.at[k - 1], dk_s.at[k], dk_r.at[k], ctx=xhi * 4 + to))
    for copy in copies:
        copy.start()
        sent.append(copy)


    @pl.when(home)
    def _():
        for i in (2, 3):
            relay_grads(i)

    for side in range(2):
        for k in range(4):
            lanes = pl.ds(
                pl.multiple_of((((xlo if side == 0 else 1 - xlo) * 4 + (y - k + 4) % 4) * 2 + other) * BLOCK, BLOCK),
                BLOCK,
            )
            arrived(at.at[:, lanes], af_r.at[side, k])
    other_kinds()

    def block_and_legs(slot):
        block_sums(slot)
        first_leg(slot)

    lax.fori_loop(core // 2, 1, each(block_and_legs), 0)
    for head in range(HEADS):
        arrived(attf.at[:, pl.ds(aligned(other * HEADS + head, HS), HS)], att_r.at[head])
    att_out = pltpu.make_async_copy(attf, att_o, w_sem.at[7])
    att_out.start()
    for head in range(HEADS):
        arrived(gq.at[:, pl.ds(aligned(other * HEADS + head, HS), HS)], gq_r.at[head])

    def spread(i, carry):
        rows = pl.ds(aligned(i, 512), 512)
        total = dot(gq[...], wq_v[rows, :], ((1,), (1,)))
        high = total.astype(BF)
        hidf[:, rows] = high
        sb[:, rows] = (total - high.astype(F32)).astype(BF)
        return carry

    lax.fori_loop(0, 7, spread, 0)

    copies[0].wait_recv()
    for k in (1, 3, 2):
        to = (z + k) % 4
        lanes = pl.ds(pl.multiple_of((xhi * 4 + to) * CHIP, CHIP), CHIP)
        dvz[to] = (acc[1, :, lanes] + dvr[to].astype(F32)).astype(BF)
        copy = send(dvz.at[to], dvzr.at[k - 1], dk_s.at[4 + k], dk_r.at[4 + k], ctx=xhi * 4 + to)
        copy.start()
        sent.append(copy)
    for k in (1, 3, 2):
        arrived(dkr.at[k - 1], dk_r.at[k])

    def over_z(half):
        total = acc[0, :, pl.ds(pl.multiple_of((half * 4 + z) * CHIP, CHIP), CHIP)]
        for k in range(3):
            total += dkr[k, half].astype(F32)
        return total

    dkx[...] = over_z(1 - xhi).astype(BF)
    dk_copy = send(dkx, dkxr, dk_s.at[4], dk_r.at[4], ctx=xctx)
    dk_copy.start()
    sent.append(dk_copy)
    @pl.when(home)
    def _():
        for i in (4, 5, 6):
            relay_grads(i)

    lax.fori_loop(1 + core // 2, 2, each(block_and_legs), 0)
    dk = over_z(xhi)
    dv = acc[1, :, pl.ds(pl.multiple_of((xhi * 4 + z) * CHIP, CHIP), CHIP)] + dvr[z].astype(F32)
    for k in (1, 3, 2):
        arrived(dvzr.at[k - 1], dk_r.at[4 + k])
    for k in range(3):
        dv += dvzr[k].astype(F32)
    gkv[1, core] = dv.T.astype(BF)
    dk_copy.wait_recv()
    dk = (dk + dkxr[...].astype(F32)) * scale
    gkv[0, core] = dk.T.astype(BF)
    gkv_copy = send(gkv.at[:, core], gkv.at[:, core], pair_s.at[4], pair_r.at[4], mod=other)
    gkv_copy.start()
    sent.append(gkv_copy)
    for i, target, slot in ((0, 0, 4), (1, 1, 3)):
        straight_out(gkv.at[i, core], target, slot, b_s.at[0, HEADS + i])

    lax.fori_loop(2, last - 1, each(block_and_legs), 0)

    arrived(gkv.at[:, other], pair_r.at[4])
    grads_kv = jnp.concatenate([gkv[0, 0], gkv[0, 1], gkv[1, 0], gkv[1, 1]], axis=1)
    for i in range(7):
        rows = slice(i * 512, (i + 1) * 512)
        total = hidf[:, rows].astype(F32) + sb[:, rows].astype(F32) + dot(grads_kv, wkv_v[rows, :], ((1,), (1,)))
        sb[:, rows] = total.astype(BF)
    home_copy = send(sb.at[other_rows], sr, pair_s.at[5], pair_r.at[5], mod=other)
    home_copy.start()
    sent.append(home_copy)
    lax.fori_loop(last - 1, last, each(block_sums), 0)
    last_first_leg()
    arrived(sr, pair_r.at[5])
    pick = jnp.broadcast_to(mods[here][0:1, 0:1], (BLOCK, D)) == expert
    ghf[...] = jnp.where(pick, sb[own_rows, :], sr[...])
    gh_out = pltpu.make_async_copy(ghf, gh_o, w_sem.at[8])
    gh_out.start()
    lax.fori_loop(0, 2, each(second_leg), 0)

    def results_out(slot):
        for s in range(2):
            for e in range(2):
                at_home = jnp.logical_and(xlo == s, core == e)

                @pl.when(at_home)
                def _():
                    pltpu.make_async_copy(
                        fin.at[slot, s, e], finr.at[xlo, core, slot], fin_r.at[xlo, core, slot]
                    ).start()

                @pl.when(jnp.logical_not(at_home))
                def _():
                    result_copy(slot, s, e).start()

    def result_copy(slot, s, e):
        return send(
            fin.at[slot, s, e], finr.at[xlo, core, slot], fin_s.at[slot, s, e], fin_r.at[xlo, core, slot],
            dp=s * 4 + y, mod=e,
        )

    def last_step(slot):
        last_leg(slot)
        results_out(slot)

    lax.fori_loop(2, last - 1, each(second_leg), 0)
    last_second_leg()
    lax.fori_loop(core // 2, last - 1, each(last_step), 0)
    last_last_leg()
    results_out(last - 1)

    att_out.wait()
    gh_out.wait()
    for g in range(2):
        for c in range(2):
            for slot in range(5 - c):
                arrived(finr.at[g, c, slot], fin_r.at[g, c, slot])

    for copy in sent:
        copy.wait_send()

    def heads_sent(head, carry):
        full_lanes = pl.ds(aligned(core * HEADS + head, HS), HS)
        send(
            attb.at[head, other_rows], attf.at[:, full_lanes], att_s.at[head], att_r.at[head], mod=other
        ).wait_send()
        send(dqb.at[head], gq.at[:, full_lanes], gq_s.at[head], gq_r.at[head], mod=other).wait_send()

        @pl.when(jnp.logical_not(home))
        def _():
            cross(head).wait_send()

        @pl.when(home)
        def _():
            fan_sent(dqb.at[head], xlo, head // 4, head % 4, b_s.at[0, head])
            fan_sent(dqx.at[head], 1 - xlo, head // 4, head % 4, b_s.at[1, head])

        return carry

    lax.fori_loop(0, HEADS, heads_sent, 0)
    for side in range(2):
        for k in range(4):
            pass_hidden(side, k).wait_send()
            if side or k:
                for s in range(2):
                    hidden_copy(side, k, s).wait_send()
    for i, target, slot in ((0, 0, 4), (1, 1, 3)):
        straight_sent(gkv.at[i, core], target, slot, b_s.at[0, HEADS + i])

    def blocks_sent(slot, carry):
        then_x(slot).wait_send()
        for k in (1, 3, 2):
            z_leg(slot, k).wait_send()

        @pl.when(slot < last - 1)
        def _():
            then_x1(slot).wait_send()
            for k in (1, 3, 2):
                z_leg1(slot, k).wait_send()

        for s in range(2):
            for e in range(2):

                @pl.when(jnp.logical_not(jnp.logical_and(xlo == s, core == e)))
                def _():
                    result_copy(slot, s, e).wait_send()

        return carry

    lax.fori_loop(0, last, blocks_sent, 0)
    x_leg().wait_send()
    for k in (1, 3, 2):
        then_z(k).wait_send()


def results(att, gh, fin, att_o, gh_o, gwq_o, gwkv_o):
    att_o[...] = att[...]
    gh_o[...] = gh[...]
    for g in range(2):
        for head in range(HEADS):
            cols = slice((g * HEADS + head) * HS, (g * HEADS + head + 1) * HS)
            gwq_o[:, cols] = fin[g, head // 4, head % 4][:PART]
        gwkv_o[:, g * HS:(g + 1) * HS] = fin[g, 0, 4][:PART]
        gwkv_o[:, KW + g * HS:KW + (g + 1) * HS] = fin[g, 1, 3][:PART]


def on_device(hidden_in, out_grad, modality, segment, w_query, w_keyval):
    vmem, dma = pltpu.VMEM, pltpu.SemaphoreType.DMA
    scratch = [
        vmem((BLOCK, D), BF), vmem((BLOCK, QW), BF), vmem((1, BLOCK), jnp.int32), vmem((1, SEQ), jnp.int32),
        vmem((BLOCK, QW), BF), vmem((BLOCK, D), BF), vmem((D, QW), BF), vmem((D, 2 * KW), BF),
        vmem((CHIP, D), BF), vmem((D, BLOCK), BF), vmem((CHIP, GW), BF), vmem((16, 8, HS), F32),
        vmem((2 * SLICE, SEQ), BF),
        vmem((2, 2, CHIP, HS), BF), vmem((2, CHIP, HS), BF), vmem((2, SEQ, HS), BF),
        vmem((2, CHIP, GW), BF), vmem((CHIP, GW), BF), vmem((CHIP, GW), BF), vmem((CHIP, SEQ), F32),
        vmem((8, BLOCK), F32), vmem((HEADS, CHIP, HS), BF), vmem((HEADS, CHIP, HS), BF), vmem((HEADS, CHIP, HS), BF), vmem((CHIP, QW), BF),
        vmem((2, HS, SEQ), F32), vmem((2, 2, 4, HS, CHIP), BF), vmem((3, 2, HS, CHIP), BF), vmem((4, HS, CHIP), BF), vmem((4, HS, CHIP), BF), vmem((3, HS, CHIP), BF),
        vmem((HS, CHIP), BF), vmem((HS, CHIP), BF), vmem((2, 2, CHIP, HS), BF),
        vmem((5, SEQ, HS), BF), vmem((SEQ, 2 * HS), BF), vmem((2 * SLICE, 2 * HS), F32),
        vmem((5, 4, 2, 2 * PART, HS), BF), vmem((5, 4, 2, 2 * PART, HS), BF), vmem((5, 3, 2, 2 * PART, HS), BF), vmem((5, 3, 2, 2 * PART, HS), BF), vmem((4, 2 * PART, HS), BF),
        vmem((5, 2, 2 * PART, HS), BF), vmem((5, 2, 2 * PART, HS), BF), vmem((4, 2 * PART, HS), BF), vmem((3, 2 * PART, HS), BF), vmem((5, 2, 2 * PART, HS), F32),
        vmem((5, 2, 2, 64, HS), BF),
        vmem((CHIP, D), BF), vmem((BLOCK, D), BF),
        dma((11,)), dma((6,)), dma((6,)), dma((8, 2)), dma((8, 2)), dma((2, 4, 2)), dma((2, 4, 2)), dma((2, 4)), dma((2, 4)),
        dma((2, 2, 4)), dma((2, 2, 4)), dma((HEADS,)), dma((HEADS,)), dma((HEADS,)), dma((HEADS,)),
        dma((HEADS,)), dma((HEADS,)), dma((2, 9, 4)), dma((5, 8)), dma((8,)), dma((8,)), dma((5, 7)), dma((5, 7)), dma((6, 4)), dma((6, 4)),
        dma((5, 2, 2)), dma((2, 2, 5)),
    ]
    in_vmem, anywhere = pl.BlockSpec(memory_space=pltpu.VMEM), pl.BlockSpec(memory_space=pl.ANY)
    raw = pl.pallas_call(
        layer,
        out_shape=(
            jax.ShapeDtypeStruct((BLOCK, QW), BF),
            jax.ShapeDtypeStruct((BLOCK, D), BF),
            jax.ShapeDtypeStruct((2, 2, 5, 64, HS), BF),
        ),
        in_specs=[anywhere] * 6,
        out_specs=(anywhere, anywhere, in_vmem),
        scratch_shapes=scratch,
        compiler_params=pltpu.CompilerParams(
            collective_id=0, has_side_effects=True, vmem_limit_bytes=63 * 2**20
        ),
        name="layer",
    )(hidden_in[0], out_grad[0], modality, segment, w_query[0], w_keyval[0])
    attended, grad_hidden, grad_wq, grad_wkv = pl.pallas_call(
        results,
        out_shape=(
            jax.ShapeDtypeStruct((BLOCK, QW), BF),
            jax.ShapeDtypeStruct((BLOCK, D), BF),
            jax.ShapeDtypeStruct((PART, QW), BF),
            jax.ShapeDtypeStruct((PART, 2 * KW), BF),
        ),
        in_specs=[in_vmem] * 3,
        out_specs=(in_vmem,) * 4,
        name="results",
    )(*raw)
    return attended[None], grad_hidden[None], grad_wq[None], grad_wkv[None]


def solution(mesh):
    return jax.shard_map(
        on_device,
        mesh=mesh,
        in_specs=(
            P("dp", ("ctx", "mod"), None),
            P("dp", ("ctx", "mod"), None),
            P("dp", ("ctx", "mod")),
            P("dp", None),
            P("mod", None, None),
            P("mod", None, None),
        ),
        out_specs=(
            P("dp", ("ctx", "mod"), None),
            P("dp", ("ctx", "mod"), None),
            P("mod", ("dp", "ctx"), None),
            P("mod", ("dp", "ctx"), None),
        ),
        check_vma=False,
    )
```

```python
import functools
import math

import jax
import jax.numpy as jnp
from jax import lax
from jax.experimental import pallas as pl
from jax.experimental.pallas import tpu as pltpu
from jax.sharding import PartitionSpec as P

HS = 128
BLOCK = 128
D = 3584
QW = 1792
KW = 256
SEQ = 2048
HEADS = 7
GW = HEADS * HS
CHIP = 2 * BLOCK
SLICE = 448
PART = 56
MESH = pl.DeviceIdType.MESH
BF = jnp.bfloat16
F32 = jnp.float32


def aligned(index, step):
    return pl.multiple_of(index * step, step)


def dot(a, b, dims=((1,), (0,))):
    return lax.dot_general(a, b, (dims, ((), ())), preferred_element_type=F32)


def send(src, dst, send_sem, recv_sem, **device):
    return pltpu.make_async_remote_copy(
        src_ref=src, dst_ref=dst, send_sem=send_sem, recv_sem=recv_sem,
        device_id=device, device_id_type=MESH,
    )


def arrived(dst, sem):
    pltpu.make_async_copy(dst, dst, sem).wait()


def layer(
    hid_h, og_h, kinds_h, segs_h, wq, wkv,
    att_o, gh_o, finr,
    hid, og, kinds, segs, attf, ghf, wq_v, wkv_v, hidf, hid_t, ogf, mods, at, kvs, kvr, kvall, qs, qr, qf, bias,
    modv, attb, dqb, dqx, gq, acc, dkvb, dkr, dvr, dvz, dvzr, dkx, dkxr, gkv, bg, be, cf, cs, cs1, crz, crx, cx, cxr, cz, czr, keep, fin, sb, sr,
    w_sem, pair_s, pair_r, mod_s, mod_r, a_s, a_r, af_s, af_r, kv_s, kv_r,
    att_s, att_r, gq_s, gq_r, bx_s, bx_r, b_s, b_r, dk_s, dk_r, c_s, c_r, cx_s, cx_r, fin_s, fin_r,
):
    dp, ctx, core = lax.axis_index("dp"), lax.axis_index("ctx"), lax.axis_index("mod")
    xlo, y, xhi, z = dp // 4, dp % 4, ctx // 4, ctx % 4
    other = 1 - core
    here = dp * 2 + core
    expert = core.astype(F32)
    scale = 1.0 / math.sqrt(HS)

    q_cols = []
    for group in (other, core):
        for first, width in ((0, 512), (512, 384)):
            q_cols.append((group, first, width))
    own_loads = [
        pltpu.make_async_copy(hid_h, hid, w_sem.at[5]), pltpu.make_async_copy(og_h, og, w_sem.at[6]),
        pltpu.make_async_copy(kinds_h, kinds, w_sem.at[9]), pltpu.make_async_copy(segs_h, segs, w_sem.at[10]),
    ]
    loads = [pltpu.make_async_copy(wkv, wkv_v, w_sem.at[0])]
    for i, (group, first, width) in enumerate(q_cols):
        cols = pl.ds(pl.multiple_of(group * GW + first, 128), width)
        loads.append(pltpu.make_async_copy(wq.at[:, cols], wq_v.at[:, cols], w_sem.at[1 + i]))
    barrier = pltpu.get_barrier_semaphore()
    for k in range(8):
        pl.semaphore_signal(barrier, inc=1, device_id={"dp": (dp + k) % 8, "mod": other}, device_id_type=MESH)
        if k:
            pl.semaphore_signal(barrier, inc=1, device_id={"dp": (dp + k) % 8}, device_id_type=MESH)
            pl.semaphore_signal(barrier, inc=1, device_id={"ctx": (ctx + k) % 8}, device_id_type=MESH)
    for load in own_loads + loads:
        load.start()
    for load in own_loads:
        load.wait()
    pl.semaphore_wait(barrier, 22)

    own_rows = pl.ds(aligned(core, BLOCK), BLOCK)
    other_rows = pl.ds(aligned(other, BLOCK), BLOCK)
    sent = []

    hid_copy = send(hid, hidf.at[own_rows], pair_s.at[0], pair_r.at[0], mod=other)
    hid_copy.start()
    og_copy = send(og.at[:, pl.ds(aligned(other, GW), GW)], ogf.at[own_rows], pair_s.at[1], pair_r.at[1], mod=other)
    og_copy.start()
    sent += [hid_copy, og_copy]
    modv[...] = jnp.broadcast_to(kinds[...].astype(F32), (8, BLOCK))
    mods[here] = modv[...]
    for k in range(8):
        for c in range(2):
            if k == 0 and c == 0:
                continue
            dev = {"dp": (dp + k) % 8, "mod": other if c else core}
            copy = send(modv, mods.at[here], mod_s, mod_r.at[1 if k else 0], **dev)
            copy.start()
    hidf[own_rows, :] = hid[...]
    ogf[own_rows, :] = og[:, pl.ds(aligned(core, GW), GW)]

    here_lanes = pl.ds(aligned(here, BLOCK), BLOCK)
    for i in range(7):
        hid_t[i * 512:(i + 1) * 512, :] = hid[:, i * 512:(i + 1) * 512].T
    def hidden_copy(side, k, s):
        to = (y + k) % 4
        rows = pl.ds(pl.multiple_of((s * 4 + to) * SLICE, 64), SLICE)
        return send(
            hid_t.at[rows], at.at[pl.ds(s * SLICE, SLICE), here_lanes], a_s, a_r.at[side, k],
            dp=(xlo if side == 0 else 1 - xlo) * 4 + to,
        )

    def send_hidden(side, k):
        for s in range(2):
            hidden_copy(side, k, s).start()

    for side, k in ((1, 0), (0, 1), (0, 3), (0, 2)):
        send_hidden(side, k)
    for s in range(2):
        rows = pl.ds(pl.multiple_of((s * 4 + y) * SLICE, 64), SLICE)
        at[s * SLICE:(s + 1) * SLICE, here_lanes] = hid_t[rows, :]

    def lanes_of(side, k):
        return pl.ds(pl.multiple_of((((xlo if side == 0 else 1 - xlo) * 4 + (y - k + 4) % 4) * 2 + core) * BLOCK, BLOCK), BLOCK)

    def pass_hidden(side, k):
        lanes = lanes_of(side, k)
        return send(at.at[:, lanes], at.at[:, lanes], af_s, af_r, mod=other)

    def relay_hidden(side, k):
        if side or k:
            arrived(at.at[:, lanes_of(side, k)], a_r.at[side, k])
        pass_hidden(side, k).start()

    loads[0].wait()

    def key_rows(rows):
        made = dot(hidf[rows, :], wkv_v[...]).astype(BF)
        for i in range(2):
            for g in range(2):
                kvs[i, g, rows, :] = made[:, (i * 2 + g) * HS:(i * 2 + g + 1) * HS]

    key_rows(own_rows)
    hid_copy.wait_recv()
    key_rows(other_rows)
    copy = send(kvs.at[:, other], kvr, pair_s.at[2], pair_r.at[2], mod=other)
    copy.start()
    sent.append(copy)
    def other_kinds():
        arrived(mods.at[0:14], mod_r.at[1])

    arrived(mods.at[dp * 2 + other], mod_r.at[0])
    mine = [
        jnp.broadcast_to(mods[dp * 2 + b][0:1, :], (BLOCK, HS)) == expert for b in range(2)
    ]
    copy.wait_recv()
    for i in range(2):
        for b in range(2):
            rows = slice(b * BLOCK, (b + 1) * BLOCK)
            kvall[i, pl.ds(pl.multiple_of(ctx * CHIP + b * BLOCK, BLOCK), BLOCK), :] = jnp.where(
                mine[b], kvs[i, core, rows, :], kvr[i, rows, :]
            )
    ctx_rows = pl.ds(aligned(ctx, CHIP), CHIP)
    xctx = (1 - xhi) * 4 + z
    xctx_rows = pl.ds(aligned(xctx, CHIP), CHIP)

    def rows_from(side, k):
        return pl.ds(aligned((xhi if side == 0 else 1 - xhi) * 4 + (z - k + 4) % 4, CHIP), CHIP)

    def send_keys(i, side, k, rows, to):
        copy = send(kvall.at[i, rows], kvall.at[i, rows], kv_s, kv_r.at[i if side and not k else 2], ctx=to)
        copy.start()

    def keys_from(i, side, k):
        arrived(kvall.at[i, rows_from(side, k)], kv_r.at[i])

    for i in range(2):
        send_keys(i, 1, 0, ctx_rows, xctx)
    for k in (1, 3, 2):
        for i in range(2):
            send_keys(i, 0, k, ctx_rows, xhi * 4 + (z + k) % 4)

    def project(i):
        group, first, width = q_cols[i]
        loads[1 + i].wait()
        cols = pl.ds(pl.multiple_of(group * GW + first, 128), width)
        qs[group, :, first:first + width] = dot(hidf[...], wq_v[:, cols]).astype(BF)

    project(0)
    for i in range(2):
        keys_from(i, 1, 0)
        for k in (1, 3, 2):
            send_keys(i, 1, k, xctx_rows, xhi * 4 + (z + k) % 4)
    for k in (2, 1, 3):
        send_hidden(1, k)
    project(1)
    q_copy = send(qs.at[other], qr, pair_s.at[3], pair_r.at[3], mod=other)
    q_copy.start()
    sent.append(q_copy)
    project(2)
    project(3)
    seg_rows = segs[:, pl.ds(aligned(ctx, CHIP), CHIP)].astype(F32)
    seg_col = jnp.broadcast_to(seg_rows, (128, CHIP)).T[:, 0:1]
    bias[...] = jnp.where(segs[...].astype(F32) <= seg_col, 0.0, -1e30)
    acc[...] = jnp.zeros_like(acc)
    q_copy.wait_recv()
    for b in range(2):
        rows = slice(b * BLOCK, (b + 1) * BLOCK)
        pick = jnp.broadcast_to(mods[dp * 2 + b][0:1, 0:1], (BLOCK, GW)) == expert
        qf[rows, :] = jnp.where(pick, qs[core, rows, :], qr[rows, :])
    og_copy.wait_recv()
    arrived(kvall.at[:, 0:6 * CHIP], kv_r.at[2])

    last = 5 - core

    def head_scores(head):
        q = qf[:, pl.ds(aligned(head, HS), HS)]
        return dot(q, kvall[0], ((1,), (1,))) * (scale * math.log2(math.e)) + bias[...]

    def rest_of_head(head, scores):
        lanes = pl.ds(aligned(head, HS), HS)
        full_lanes = pl.ds(aligned(core * HEADS + head, HS), HS)
        q, go = qf[:, lanes], ogf[:, lanes]
        keys, values = kvall[0], kvall[1]
        top = jnp.max(scores, axis=1, keepdims=True)
        weights = jnp.exp2(scores - top)
        total = jnp.sum(weights, axis=1, keepdims=True)
        low = weights.astype(BF)
        inv = 1.0 / total
        attended = (dot(low, values) * inv).astype(BF)
        attb[head] = attended
        copy = send(
            attb.at[head, other_rows], attf.at[:, full_lanes], att_s, att_r, mod=other
        )
        copy.start()
        attf[:, full_lanes] = attb[head, own_rows, :]
        go32 = go.astype(F32)
        delta = jnp.sum(go32 * attended.astype(F32), axis=1, keepdims=True)
        dprob = dot(go, values, ((1,), (1,)))
        dscore = (weights * (dprob * inv - delta * inv)).astype(BF)
        dq = (dot(dscore, keys) * scale).astype(BF)
        dqb[head] = dq
        gq[:, full_lanes] = dq
        copy = send(dqb.at[head], gq.at[:, full_lanes], gq_s, gq_r, mod=other)
        copy.start()
        acc[0] += dot(q.T, dscore)
        acc[1] += dot((go32 * inv).astype(BF).T, low)

    def two_heads(p, carry):
        first, second = head_scores(p), head_scores(4 + p)
        rest_of_head(p, first)
        rest_of_head(4 + p, second)
        spread_grads(p, 0, p)
        spread_grads(4 + p, 1, p)

        @pl.when(jnp.logical_and(home, p == 2))
        def _():
            relay_grads(0)
            relay_grads(1)

        @pl.when(p == 1)
        def _():
            for k in range(4):
                relay_hidden(0, k)

        @pl.when(p == 2)
        def _():
            for k in (0, 2, 1, 3):
                relay_hidden(1, k)

        return carry

    home = xlo == core

    def cross(head):
        return send(dqb.at[head], dqx.at[head], bx_s, bx_r.at[head], dp=(1 - xlo) * 4 + y)

    def straight(src, target, slot, sems, k):
        rows = pl.ds(aligned(dp, CHIP), CHIP)
        return send(
            src, bg.at[slot, rows], sems, b_r.at[slot], dp=core * 4 + (y + k) % 4, mod=target
        )

    def straight_out(src, target, slot, sems):
        at_home = jnp.logical_and(home, target == core)
        rows = pl.ds(aligned(dp, CHIP), CHIP)
        for k in (1, 3, 2):
            straight(src, target, slot, sems, k).start()

        @pl.when(at_home)
        def _():
            pltpu.make_async_copy(src, bg.at[slot, rows], b_r.at[slot]).start()

        @pl.when(jnp.logical_not(at_home))
        def _():
            straight(src, target, slot, sems, 0).start()

    def fan(src, side, target, slot, sems, k):
        rows = pl.ds(pl.multiple_of((side * 4 + y) * CHIP, CHIP), CHIP)
        return send(
            src, bg.at[slot, rows], sems, b_r.at[slot], dp=xlo * 4 + (y + k) % 4, mod=target
        )

    def fan_out(src, side, target, slot, sems):
        rows = pl.ds(pl.multiple_of((side * 4 + y) * CHIP, CHIP), CHIP)
        for k in (1, 3, 2):
            fan(src, side, target, slot, sems, k).start()

        @pl.when(target == core)
        def _():
            pltpu.make_async_copy(src, bg.at[slot, rows], b_r.at[slot]).start()

        @pl.when(target != core)
        def _():
            fan(src, side, target, slot, sems, 0).start()

    def relay_grads(i):
        slot, target = i // 2, i % 2
        head = target * 4 + slot
        arrived(dqx.at[head], bx_r.at[head])
        fan_out(dqx.at[head], 1 - xlo, target, slot, b_s.at[1])

    def spread_grads(head, target, slot):
        @pl.when(jnp.logical_not(home))
        def _():
            cross(head).start()

        @pl.when(home)
        def _():
            fan_out(dqb.at[head], xlo, target, slot, b_s.at[0])

    def block_sums(slot):
        arrived(bg.at[slot], b_r.at[slot])
        for t in range(16):
            rows = slice(t * BLOCK, (t + 1) * BLOCK)
            kind = mods[t][0:1, :]
            block = bg[slot, rows, :]
            second = jnp.where(jnp.broadcast_to(kind, (BLOCK, HS)) == 1.0, block, jnp.zeros_like(block))
            be[rows, HS:] = second
            be[rows, :HS] = block - second
        cf[...] = dot(at[...], be[...])
        for c in range(8):
            for e, buf in enumerate((cs, cs1)):
                cols = slice(e * HS, (e + 1) * HS)
                both = jnp.concatenate(
                    [cf[c * PART:(c + 1) * PART, cols], cf[SLICE + c * PART:SLICE + (c + 1) * PART, cols]], axis=0
                )
                buf[slot, c % 4, c // 4] = both.astype(BF)

    def z_leg(slot, k):
        to = (z + k) % 4
        return send(cs.at[slot, to], crz.at[slot, k - 1], c_s.at[slot], c_r.at[slot, 1], ctx=xhi * 4 + to)

    def x_leg(slot):
        return send(cs1.at[slot, :, 1 - xhi], crx.at[slot], c_s.at[slot], c_r.at[slot, 0], ctx=xctx)

    def then_x(slot):
        return send(cx.at[slot], cxr.at[slot], cx_s.at[slot], cx_r.at[slot, 0], ctx=xctx)

    def then_z(slot, k):
        to = (z + k) % 4
        return send(cz.at[slot, to], czr.at[slot, k - 1], cx_s.at[slot], cx_r.at[slot, 1], ctx=xhi * 4 + to)

    def first_leg(slot):
        x_leg(slot).start()
        for k in (1, 3, 2):
            z_leg(slot, k).start()

    def second_leg(slot):
        arrived(crx.at[slot], c_r.at[slot, 0])
        for k in (1, 3, 2):
            to = (z + k) % 4
            cz[slot, to] = (cs1[slot, to, xhi].astype(F32) + crx[slot, to].astype(F32)).astype(BF)
            then_z(slot, k).start()
        keep[slot, 1] = cs1[slot, z, xhi].astype(F32) + crx[slot, z].astype(F32)
        arrived(crz.at[slot], c_r.at[slot, 1])
        total = cs[slot, z, 1 - xhi].astype(F32)
        for k in range(3):
            total += crz[slot, k, 1 - xhi].astype(F32)
        cx[slot] = total.astype(BF)
        then_x(slot).start()
        total = cs[slot, z, xhi].astype(F32)
        for k in range(3):
            total += crz[slot, k, xhi].astype(F32)
        keep[slot, 0] = total

    def finish(slot, totals):
        for e, total in enumerate(totals):
            for s in range(2):
                padded = jnp.concatenate([total[s * PART:(s + 1) * PART], jnp.zeros((8, HS), F32)], axis=0)
                fin[slot, s, e] = padded.astype(BF)

    def last_leg(slot):
        arrived(cxr.at[slot], cx_r.at[slot, 0])
        second = keep[slot, 1]
        arrived(czr.at[slot], cx_r.at[slot, 1])
        for k in range(3):
            second += czr[slot, k].astype(F32)
        finish(slot, [keep[slot, 0] + cxr[slot].astype(F32), second])

    def each(step):
        def run(slot, carry):
            step(slot)
            return carry

        return run

    lax.fori_loop(0, 3, two_heads, 0)
    rest_of_head(3, head_scores(3))
    spread_grads(3, 0, 3)

    for c in range(8):
        for i in range(2):
            dkvb[i, c // 4, c % 4] = acc[i, :, c * CHIP:(c + 1) * CHIP].astype(BF)
    copies = [send(dkvb.at[1, 1 - xhi], dvr, dk_s.at[0], dk_r.at[0], ctx=xctx)]
    for k in (1, 3, 2):
        to = (z + k) % 4
        copies.append(send(dkvb.at[0, :, to], dkr.at[k - 1], dk_s.at[1], dk_r.at[1], ctx=xhi * 4 + to))
    for copy in copies:
        copy.start()


    @pl.when(home)
    def _():
        for i in (2, 3):
            relay_grads(i)

    arrived(attf.at[:, pl.ds(aligned(other, GW), GW)], att_r)
    att_out = pltpu.make_async_copy(attf, att_o, w_sem.at[7])
    att_out.start()
    arrived(gq.at[:, pl.ds(aligned(other, GW), GW)], gq_r)

    def spread(i, carry):
        rows = pl.ds(aligned(i, 512), 512)
        total = dot(gq[...], wq_v[rows, :], ((1,), (1,)))
        high = total.astype(BF)
        hidf[:, rows] = high
        sb[:, rows] = (total - high.astype(F32)).astype(BF)
        return carry

    lax.fori_loop(0, 7, spread, 0)
    arrived(at.at[:, 0:8 * BLOCK], af_r)
    other_kinds()

    def block_and_legs(slot):
        block_sums(slot)
        first_leg(slot)

    lax.fori_loop(core // 2, 1, each(block_sums), 0)

    copies[0].wait_recv()
    for k in (1, 3, 2):
        to = (z + k) % 4
        lanes = pl.ds(pl.multiple_of((xhi * 4 + to) * CHIP, CHIP), CHIP)
        dvz[to] = (acc[1, :, lanes] + dvr[to].astype(F32)).astype(BF)
        copy = send(dvz.at[to], dvzr.at[k - 1], dk_s.at[0], dk_r.at[2], ctx=xhi * 4 + to)
        copy.start()
    arrived(dkr, dk_r.at[1])

    def over_z(half):
        total = acc[0, :, pl.ds(pl.multiple_of((half * 4 + z) * CHIP, CHIP), CHIP)]
        for k in range(3):
            total += dkr[k, half].astype(F32)
        return total

    dkx[...] = over_z(1 - xhi).astype(BF)
    dk_copy = send(dkx, dkxr, dk_s.at[0], dk_r.at[3], ctx=xctx)
    dk_copy.start()
    first_leg(0)
    lax.fori_loop(1 + core // 2, 2, each(block_and_legs), 0)
    @pl.when(home)
    def _():
        for i in (4, 5, 6):
            relay_grads(i)

    dk = over_z(xhi)
    dv = acc[1, :, pl.ds(pl.multiple_of((xhi * 4 + z) * CHIP, CHIP), CHIP)] + dvr[z].astype(F32)
    arrived(dvzr, dk_r.at[2])
    for k in range(3):
        dv += dvzr[k].astype(F32)
    gkv[1, core] = dv.T.astype(BF)
    dk_copy.wait_recv()
    dk = (dk + dkxr[...].astype(F32)) * scale
    gkv[0, core] = dk.T.astype(BF)
    gkv_copy = send(gkv.at[:, core], gkv.at[:, core], pair_s.at[4], pair_r.at[4], mod=other)
    gkv_copy.start()
    sent.append(gkv_copy)
    for i, target, slot in ((0, 0, 4), (1, 1, 3)):
        straight_out(gkv.at[i, core], target, slot, b_s.at[2])

    lax.fori_loop(2, last - 1, each(block_and_legs), 0)

    arrived(gkv.at[:, other], pair_r.at[4])
    grads_kv = jnp.concatenate([gkv[0, 0], gkv[0, 1], gkv[1, 0], gkv[1, 1]], axis=1)
    for i in range(7):
        rows = slice(i * 512, (i + 1) * 512)
        total = hidf[:, rows].astype(F32) + sb[:, rows].astype(F32) + dot(grads_kv, wkv_v[rows, :], ((1,), (1,)))
        sb[:, rows] = total.astype(BF)
    home_copy = send(sb.at[other_rows], sr, pair_s.at[5], pair_r.at[5], mod=other)
    home_copy.start()
    sent.append(home_copy)
    lax.fori_loop(last - 1, last, each(block_and_legs), 0)
    arrived(sr, pair_r.at[5])
    pick = jnp.broadcast_to(mods[here][0:1, 0:1], (BLOCK, D)) == expert
    ghf[...] = jnp.where(pick, sb[own_rows, :], sr[...])
    gh_out = pltpu.make_async_copy(ghf, gh_o, w_sem.at[8])
    gh_out.start()
    lax.fori_loop(0, 2, each(second_leg), 0)

    def results_out(slot):
        for s in range(2):
            for e in range(2):
                at_home = jnp.logical_and(xlo == s, core == e)

                @pl.when(at_home)
                def _():
                    pltpu.make_async_copy(
                        fin.at[slot, s, e], finr.at[xlo, core, slot], fin_r.at[core]
                    ).start()

                @pl.when(jnp.logical_not(at_home))
                def _():
                    result_copy(slot, s, e).start()

    def result_copy(slot, s, e):
        return send(
            fin.at[slot, s, e], finr.at[xlo, core, slot], fin_s.at[slot], fin_r.at[core],
            dp=s * 4 + y, mod=e,
        )

    def last_step(slot):
        last_leg(slot)
        results_out(slot)

    lax.fori_loop(2, last, each(second_leg), 0)
    lax.fori_loop(core // 2, last, each(last_step), 0)

    att_out.wait()
    gh_out.wait()
    arrived(finr.at[:, 0], fin_r.at[0])
    arrived(finr.at[:, 1, 0:4], fin_r.at[1])

    for copy in sent:
        copy.wait_send()

    arrived(attf.at[:, 0:GW], att_s)
    arrived(gq.at[:, 0:GW], gq_s)
    arrived(mods.at[0:15], mod_s)
    arrived(kvall.at[:, 0:7 * CHIP], kv_s)
    arrived(at.at[:, 0:8 * BLOCK], af_s)
    arrived(at.at[:, 0:7 * BLOCK], a_s)
    arrived(dkvb.at[0], dk_s.at[0])
    arrived(dkr, dk_s.at[1])

    @pl.when(jnp.logical_not(home))
    def _():
        arrived(dqb, bx_s)
        arrived(bg.at[0], b_s.at[2])

    @pl.when(home)
    def _():
        arrived(bg.at[0, 0:7 * CHIP], b_s.at[2])
        for side in range(2):
            @pl.when(core == 0)
            def _():
                arrived(bg.at[0:3], b_s.at[side])

            @pl.when(core == 1)
            def _():
                arrived(bg.at[:, 0:5 * CHIP], b_s.at[side])

    def blocks_sent(slot, carry):
        arrived(cs.at[:, 0], c_s.at[slot])
        arrived(cz.at[slot], cx_s.at[slot])
        arrived(finr.at[0, 0, 0:3], fin_s.at[slot])
        return carry

    lax.fori_loop(0, last, blocks_sent, 0)


def results(att, gh, fin, att_o, gh_o, gwq_o, gwkv_o):
    att_o[...] = att[...]
    gh_o[...] = gh[...]
    for g in range(2):
        for head in range(HEADS):
            cols = slice((g * HEADS + head) * HS, (g * HEADS + head + 1) * HS)
            gwq_o[:, cols] = fin[g, head // 4, head % 4][:PART]
        gwkv_o[:, g * HS:(g + 1) * HS] = fin[g, 0, 4][:PART]
        gwkv_o[:, KW + g * HS:KW + (g + 1) * HS] = fin[g, 1, 3][:PART]


def on_device(hidden_in, out_grad, modality, segment, w_query, w_keyval):
    vmem, dma = pltpu.VMEM, pltpu.SemaphoreType.DMA
    scratch = [
        vmem((BLOCK, D), BF), vmem((BLOCK, QW), BF), vmem((1, BLOCK), jnp.int32), vmem((1, SEQ), jnp.int32),
        vmem((BLOCK, QW), BF), vmem((BLOCK, D), BF), vmem((D, QW), BF), vmem((D, 2 * KW), BF),
        vmem((CHIP, D), BF), vmem((D, BLOCK), BF), vmem((CHIP, GW), BF), vmem((16, 8, HS), F32),
        vmem((2 * SLICE, SEQ), BF),
        vmem((2, 2, CHIP, HS), BF), vmem((2, CHIP, HS), BF), vmem((2, SEQ, HS), BF),
        vmem((2, CHIP, GW), BF), vmem((CHIP, GW), BF), vmem((CHIP, GW), BF), vmem((CHIP, SEQ), F32),
        vmem((8, BLOCK), F32), vmem((HEADS, CHIP, HS), BF), vmem((HEADS, CHIP, HS), BF), vmem((HEADS, CHIP, HS), BF), vmem((CHIP, QW), BF),
        vmem((2, HS, SEQ), F32), vmem((2, 2, 4, HS, CHIP), BF), vmem((3, 2, HS, CHIP), BF), vmem((4, HS, CHIP), BF), vmem((4, HS, CHIP), BF), vmem((3, HS, CHIP), BF),
        vmem((HS, CHIP), BF), vmem((HS, CHIP), BF), vmem((2, 2, CHIP, HS), BF),
        vmem((5, SEQ, HS), BF), vmem((SEQ, 2 * HS), BF), vmem((2 * SLICE, 2 * HS), F32),
        vmem((5, 4, 2, 2 * PART, HS), BF), vmem((5, 4, 2, 2 * PART, HS), BF), vmem((5, 3, 2, 2 * PART, HS), BF), vmem((5, 4, 2 * PART, HS), BF),
        vmem((5, 2 * PART, HS), BF), vmem((5, 2 * PART, HS), BF), vmem((5, 4, 2 * PART, HS), BF), vmem((5, 3, 2 * PART, HS), BF), vmem((5, 2, 2 * PART, HS), F32),
        vmem((5, 2, 2, 64, HS), BF),
        vmem((CHIP, D), BF), vmem((BLOCK, D), BF),
        dma((11,)), dma((6,)), dma((6,)), dma(()), dma((2,)), dma(()), dma((2, 4)), dma(()), dma(()),
        dma(()), dma((3,)), dma(()), dma(()), dma(()), dma(()),
        dma(()), dma((HEADS,)), dma((3,)), dma((5,)), dma((2,)), dma((4,)), dma((5,)), dma((5, 2)), dma((5,)), dma((5, 2)),
        dma((5,)), dma((2,)),
    ]
    in_vmem, anywhere = pl.BlockSpec(memory_space=pltpu.VMEM), pl.BlockSpec(memory_space=pl.ANY)
    raw = pl.pallas_call(
        layer,
        out_shape=(
            jax.ShapeDtypeStruct((BLOCK, QW), BF),
            jax.ShapeDtypeStruct((BLOCK, D), BF),
            jax.ShapeDtypeStruct((2, 2, 5, 64, HS), BF),
        ),
        in_specs=[anywhere] * 6,
        out_specs=(anywhere, anywhere, in_vmem),
        scratch_shapes=scratch,
        compiler_params=pltpu.CompilerParams(
            collective_id=0, has_side_effects=True, vmem_limit_bytes=63 * 2**20
        ),
        name="layer",
    )(hidden_in[0], out_grad[0], modality, segment, w_query[0], w_keyval[0])
    attended, grad_hidden, grad_wq, grad_wkv = pl.pallas_call(
        results,
        out_shape=(
            jax.ShapeDtypeStruct((BLOCK, QW), BF),
            jax.ShapeDtypeStruct((BLOCK, D), BF),
            jax.ShapeDtypeStruct((PART, QW), BF),
            jax.ShapeDtypeStruct((PART, 2 * KW), BF),
        ),
        in_specs=[in_vmem] * 3,
        out_specs=(in_vmem,) * 4,
        name="results",
    )(*raw)
    return attended[None], grad_hidden[None], grad_wq[None], grad_wkv[None]


def solution(mesh):
    return jax.shard_map(
        on_device,
        mesh=mesh,
        in_specs=(
            P("dp", ("ctx", "mod"), None),
            P("dp", ("ctx", "mod"), None),
            P("dp", ("ctx", "mod")),
            P("dp", None),
            P("mod", None, None),
            P("mod", None, None),
        ),
        out_specs=(
            P("dp", ("ctx", "mod"), None),
            P("dp", ("ctx", "mod"), None),
            P("mod", ("dp", "ctx"), None),
            P("mod", ("dp", "ctx"), None),
        ),
        check_vma=False,
    )
```

```python
import functools
import math

import jax
import jax.numpy as jnp
from jax import lax
from jax.experimental import pallas as pl
from jax.experimental.pallas import tpu as pltpu
from jax.sharding import PartitionSpec as P

HS = 128
BLOCK = 128
D = 3584
QW = 1792
KW = 256
SEQ = 2048
HEADS = 7
GW = HEADS * HS
CHIP = 2 * BLOCK
SLICE = 448
PART = 56
MESH = pl.DeviceIdType.MESH
BF = jnp.bfloat16
F32 = jnp.float32


def aligned(index, step):
    return pl.multiple_of(index * step, step)


def dot(a, b, dims=((1,), (0,))):
    return lax.dot_general(a, b, (dims, ((), ())), preferred_element_type=F32)


def send(src, dst, send_sem, recv_sem, **device):
    return pltpu.make_async_remote_copy(
        src_ref=src, dst_ref=dst, send_sem=send_sem, recv_sem=recv_sem,
        device_id=device, device_id_type=MESH,
    )


def arrived(dst, sem):
    pltpu.make_async_copy(dst, dst, sem).wait()


def layer(
    hid_h, og_h, kinds_h, segs_h, wq, wkv,
    att_o, gh_o, finr,
    hid, og, kinds, segs, attf, ghf, wq_v, wkv_v, hidf, hid_t, ogf, mods, at, kvs, kvr, kvall, qs, qr, qf, bias,
    modv, attb, dqb, dqx, gq, acc, dkvb, dkr, dvr, dvz, dvzr, dkx, dkxr, gkv, gkvx, bg, be, cf, cs, cs1, crz, crx, cx, cxr, cz, czr, cl, crl, keep, fin, sb, sr,
    w_sem, pair_s, pair_r, mod_s, mod_r, a_s, a_r, af_s, af_r, kv_s, kv_r,
    att_s, att_r, gq_s, gq_r, bx_s, bx_r, kx, b_s, b_r, dk_s, dk_r, c_s, c_r, cx_s, cx_r, cl_s, cl_r, fin_s, fin_r,
):
    dp, ctx, core = lax.axis_index("dp"), lax.axis_index("ctx"), lax.axis_index("mod")
    xlo, y, xhi, z = dp // 4, dp % 4, ctx // 4, ctx % 4
    other = 1 - core
    here = dp * 2 + core
    expert = core.astype(F32)
    scale = 1.0 / math.sqrt(HS)

    q_cols = []
    for group in (other, core):
        for first, width in ((0, 512), (512, 384)):
            q_cols.append((group, first, width))
    own_loads = [
        pltpu.make_async_copy(hid_h, hid, w_sem.at[5]), pltpu.make_async_copy(og_h, og, w_sem.at[6]),
        pltpu.make_async_copy(kinds_h, kinds, w_sem.at[9]), pltpu.make_async_copy(segs_h, segs, w_sem.at[10]),
    ]
    loads = [pltpu.make_async_copy(wkv, wkv_v, w_sem.at[0])]
    for i, (group, first, width) in enumerate(q_cols):
        cols = pl.ds(pl.multiple_of(group * GW + first, 128), width)
        loads.append(pltpu.make_async_copy(wq.at[:, cols], wq_v.at[:, cols], w_sem.at[1 + i]))
    barrier = pltpu.get_barrier_semaphore()
    for k in range(8):
        pl.semaphore_signal(barrier, inc=1, device_id={"dp": (dp + k) % 8, "mod": other}, device_id_type=MESH)
        if k:
            pl.semaphore_signal(barrier, inc=1, device_id={"dp": (dp + k) % 8}, device_id_type=MESH)
            for side in range(2):
                for c in range(2):
                    to = {"dp": (1 - xlo if side else xlo) * 4 + y, "ctx": (ctx + k) % 8, "mod": other if c else core}
                    pl.semaphore_signal(barrier, inc=1, device_id=to, device_id_type=MESH)
    for load in own_loads + loads:
        load.start()
    for load in own_loads:
        load.wait()
    pl.semaphore_wait(barrier, 43)

    own_rows = pl.ds(aligned(core, BLOCK), BLOCK)
    other_rows = pl.ds(aligned(other, BLOCK), BLOCK)
    sent = []

    hid_copy = send(hid, hidf.at[own_rows], pair_s.at[0], pair_r.at[0], mod=other)
    hid_copy.start()
    og_copy = send(og.at[:, pl.ds(aligned(other, GW), GW)], ogf.at[own_rows], pair_s.at[1], pair_r.at[1], mod=other)
    og_copy.start()
    sent += [hid_copy, og_copy]
    modv[...] = jnp.broadcast_to(kinds[...].astype(F32), (8, BLOCK))
    mods[here] = modv[...]
    for k in range(8):
        for c in range(2):
            if k == 0 and c == 0:
                continue
            dev = {"dp": (dp + k) % 8, "mod": other if c else core}
            copy = send(modv, mods.at[here], mod_s, mod_r.at[1 if k else 0], **dev)
            copy.start()
    hidf[own_rows, :] = hid[...]
    ogf[own_rows, :] = og[:, pl.ds(aligned(core, GW), GW)]

    here_lanes = pl.ds(aligned(here, BLOCK), BLOCK)
    for i in range(7):
        hid_t[i * 512:(i + 1) * 512, :] = hid[:, i * 512:(i + 1) * 512].T
    def hidden_copy(side, k, s):
        to = (y + k) % 4
        rows = pl.ds(pl.multiple_of((s * 4 + to) * SLICE, 64), SLICE)
        return send(
            hid_t.at[rows], at.at[pl.ds(s * SLICE, SLICE), here_lanes], a_s, a_r.at[side, k],
            dp=(xlo if side == 0 else 1 - xlo) * 4 + to,
        )

    def send_hidden(side, k):
        for s in range(2):
            hidden_copy(side, k, s).start()

    for side, k in ((1, 0), (0, 1), (0, 3), (0, 2)):
        send_hidden(side, k)
    for s in range(2):
        rows = pl.ds(pl.multiple_of((s * 4 + y) * SLICE, 64), SLICE)
        at[s * SLICE:(s + 1) * SLICE, here_lanes] = hid_t[rows, :]

    def lanes_of(side, k):
        return pl.ds(pl.multiple_of((((xlo if side == 0 else 1 - xlo) * 4 + (y - k + 4) % 4) * 2 + core) * BLOCK, BLOCK), BLOCK)

    def pass_hidden(side, k):
        lanes = lanes_of(side, k)
        return send(at.at[:, lanes], at.at[:, lanes], af_s, af_r, mod=other)

    def relay_hidden(side, k):
        if side or k:
            arrived(at.at[:, lanes_of(side, k)], a_r.at[side, k])
        pass_hidden(side, k).start()

    loads[0].wait()

    def key_rows(rows):
        made = dot(hidf[rows, :], wkv_v[...]).astype(BF)
        for i in range(2):
            for g in range(2):
                kvs[i, g, rows, :] = made[:, (i * 2 + g) * HS:(i * 2 + g + 1) * HS]

    key_rows(own_rows)
    hid_copy.wait_recv()
    key_rows(other_rows)
    copy = send(kvs.at[:, other], kvr, pair_s.at[2], pair_r.at[2], mod=other)
    copy.start()
    sent.append(copy)
    def other_kinds():
        arrived(mods.at[0:14], mod_r.at[1])

    arrived(mods.at[dp * 2 + other], mod_r.at[0])
    mine = [
        jnp.broadcast_to(mods[dp * 2 + b][0:1, :], (BLOCK, HS)) == expert for b in range(2)
    ]
    copy.wait_recv()
    for i in range(2):
        for b in range(2):
            rows = slice(b * BLOCK, (b + 1) * BLOCK)
            kvall[i, pl.ds(pl.multiple_of(ctx * CHIP + b * BLOCK, BLOCK), BLOCK), :] = jnp.where(
                mine[b], kvs[i, core, rows, :], kvr[i, rows, :]
            )
    ctx_rows = pl.ds(aligned(ctx, CHIP), CHIP)
    xctx = (1 - xhi) * 4 + z
    xctx_rows = pl.ds(aligned(xctx, CHIP), CHIP)

    def rows_from(side, k):
        return pl.ds(aligned((xhi if side == 0 else 1 - xhi) * 4 + (z - k + 4) % 4, CHIP), CHIP)

    def send_keys(i, side, k, rows, to):
        copy = send(kvall.at[i, rows], kvall.at[i, rows], kv_s, kv_r.at[i if side and not k else 2], ctx=to)
        copy.start()

    def keys_from(i, side, k):
        arrived(kvall.at[i, rows_from(side, k)], kv_r.at[i])

    for i in range(2):
        send_keys(i, 1, 0, ctx_rows, xctx)
    for k in (1, 3, 2):
        for i in range(2):
            send_keys(i, 0, k, ctx_rows, xhi * 4 + (z + k) % 4)

    def project(i):
        group, first, width = q_cols[i]
        loads[1 + i].wait()
        cols = pl.ds(pl.multiple_of(group * GW + first, 128), width)
        qs[group, :, first:first + width] = dot(hidf[...], wq_v[:, cols]).astype(BF)

    project(0)
    for i in range(2):
        keys_from(i, 1, 0)
        for k in (1, 3, 2):
            send_keys(i, 1, k, xctx_rows, xhi * 4 + (z + k) % 4)
    for k in (2, 1, 3):
        send_hidden(1, k)
    project(1)
    q_copy = send(qs.at[other], qr, pair_s.at[3], pair_r.at[3], mod=other)
    q_copy.start()
    sent.append(q_copy)
    project(2)
    project(3)
    seg_rows = segs[:, pl.ds(aligned(ctx, CHIP), CHIP)].astype(F32)
    seg_col = jnp.broadcast_to(seg_rows, (128, CHIP)).T[:, 0:1]
    bias[...] = jnp.where(segs[...].astype(F32) <= seg_col, 0.0, -1e30)
    acc[...] = jnp.zeros_like(acc)
    q_copy.wait_recv()
    for b in range(2):
        rows = slice(b * BLOCK, (b + 1) * BLOCK)
        pick = jnp.broadcast_to(mods[dp * 2 + b][0:1, 0:1], (BLOCK, GW)) == expert
        qf[rows, :] = jnp.where(pick, qs[core, rows, :], qr[rows, :])
    og_copy.wait_recv()
    arrived(kvall.at[:, 0:6 * CHIP], kv_r.at[2])

    last = 5 - core

    def head_scores(head):
        q = qf[:, pl.ds(aligned(head, HS), HS)]
        return dot(q, kvall[0], ((1,), (1,))) * (scale * math.log2(math.e)) + bias[...]

    def rest_of_head(head, scores):
        lanes = pl.ds(aligned(head, HS), HS)
        full_lanes = pl.ds(aligned(core * HEADS + head, HS), HS)
        q, go = qf[:, lanes], ogf[:, lanes]
        keys, values = kvall[0], kvall[1]
        top = jnp.max(scores, axis=1, keepdims=True)
        weights = jnp.exp2(scores - top)
        total = jnp.sum(weights, axis=1, keepdims=True)
        low = weights.astype(BF)
        inv = 1.0 / total
        attended = (dot(low, values) * inv).astype(BF)
        attb[head] = attended
        copy = send(
            attb.at[head, other_rows], attf.at[:, full_lanes], att_s, att_r, mod=other
        )
        copy.start()
        attf[:, full_lanes] = attb[head, own_rows, :]
        go32 = go.astype(F32)
        delta = jnp.sum(go32 * attended.astype(F32), axis=1, keepdims=True)
        dprob = dot(go, values, ((1,), (1,)))
        dscore = (weights * (dprob * inv - delta * inv)).astype(BF)
        dq = (dot(dscore, keys) * scale).astype(BF)
        dqb[head] = dq
        gq[:, full_lanes] = dq
        copy = send(dqb.at[head], gq.at[:, full_lanes], gq_s, gq_r, mod=other)
        copy.start()
        acc[0] += dot(q.T, dscore)
        acc[1] += dot((go32 * inv).astype(BF).T, low)

    def two_heads(p, carry):
        first, second = head_scores(p), head_scores(4 + p)
        rest_of_head(p, first)
        rest_of_head(4 + p, second)
        spread_grads(p, 0, p)
        spread_grads(4 + p, 1, p)

        @pl.when(jnp.logical_and(home, p == 2))
        def _():
            relay_grads(0)
            relay_grads(1)

        @pl.when(p == 1)
        def _():
            for k in range(4):
                relay_hidden(0, k)

        @pl.when(p == 2)
        def _():
            for k in (0, 2, 1, 3):
                relay_hidden(1, k)

        return carry

    home = xlo == core

    def cross(head):
        return send(dqb.at[head], dqx.at[head], bx_s, bx_r.at[head], dp=(1 - xlo) * 4 + y)

    def cross_kv():
        return send(gkv.at[:, core], gkvx, kx.at[0], kx.at[1], dp=(1 - xlo) * 4 + y)

    def fan(src, side, target, slot, sems, k):
        rows = pl.ds(pl.multiple_of((side * 4 + y) * CHIP, CHIP), CHIP)
        return send(
            src, bg.at[slot, rows], sems, b_r.at[slot], dp=xlo * 4 + (y + k) % 4, mod=target
        )

    def fan_out(src, side, target, slot, sems):
        rows = pl.ds(pl.multiple_of((side * 4 + y) * CHIP, CHIP), CHIP)
        for k in (1, 3, 2):
            fan(src, side, target, slot, sems, k).start()

        @pl.when(target == core)
        def _():
            pltpu.make_async_copy(src, bg.at[slot, rows], b_r.at[slot]).start()

        @pl.when(target != core)
        def _():
            fan(src, side, target, slot, sems, 0).start()

    def relay_grads(i):
        slot, target = i // 2, i % 2
        head = target * 4 + slot
        arrived(dqx.at[head], bx_r.at[head])
        fan_out(dqx.at[head], 1 - xlo, target, slot, b_s.at[1])

    def spread_grads(head, target, slot):
        @pl.when(jnp.logical_not(home))
        def _():
            cross(head).start()

        @pl.when(home)
        def _():
            fan_out(dqb.at[head], xlo, target, slot, b_s.at[0])

    def products(slot):
        arrived(bg.at[slot], b_r.at[slot])
        for t in range(16):
            rows = slice(t * BLOCK, (t + 1) * BLOCK)
            kind = mods[t][0:1, :]
            block = bg[slot, rows, :]
            second = jnp.where(jnp.broadcast_to(kind, (BLOCK, HS)) == 1.0, block, jnp.zeros_like(block))
            be[rows, HS:] = second
            be[rows, :HS] = block - second
        cf[...] = dot(at[...], be[...])

    def block_sums(slot):
        products(slot)
        for c in range(8):
            for e, buf in enumerate((cs, cs1)):
                cols = slice(e * HS, (e + 1) * HS)
                both = jnp.concatenate(
                    [cf[c * PART:(c + 1) * PART, cols], cf[SLICE + c * PART:SLICE + (c + 1) * PART, cols]], axis=0
                )
                buf[slot, c % 4, c // 4] = both.astype(BF)

    def z_leg(slot, k):
        to = (z + k) % 4
        return send(cs.at[slot, to], crz.at[slot, k - 1], c_s.at[slot], c_r.at[slot, 1], ctx=xhi * 4 + to)

    def x_leg(slot):
        return send(cs1.at[slot, :, 1 - xhi], crx.at[slot], c_s.at[slot], c_r.at[slot, 0], ctx=xctx)

    def then_x(slot):
        return send(cx.at[slot], cxr.at[slot], cx_s.at[slot], cx_r.at[slot, 0], ctx=xctx)

    def then_z(slot, k):
        to = (z + k) % 4
        return send(cz.at[slot, to], czr.at[slot, k - 1], cx_s.at[slot], cx_r.at[slot, 1], ctx=xhi * 4 + to)

    def first_leg(slot):
        x_leg(slot).start()
        for k in (1, 3, 2):
            z_leg(slot, k).start()

    def second_leg(slot):
        arrived(crx.at[slot], c_r.at[slot, 0])
        for k in (1, 3, 2):
            to = (z + k) % 4
            cz[slot, to] = (cs1[slot, to, xhi].astype(F32) + crx[slot, to].astype(F32)).astype(BF)
            then_z(slot, k).start()
        keep[slot, 1] = cs1[slot, z, xhi].astype(F32) + crx[slot, z].astype(F32)
        arrived(crz.at[slot], c_r.at[slot, 1])
        total = cs[slot, z, 1 - xhi].astype(F32)
        for k in range(3):
            total += crz[slot, k, 1 - xhi].astype(F32)
        cx[slot] = total.astype(BF)
        then_x(slot).start()
        total = cs[slot, z, xhi].astype(F32)
        for k in range(3):
            total += crz[slot, k, xhi].astype(F32)
        keep[slot, 0] = total

    def straight_parts():
        for c in range(8):
            for e in range(2):
                for s in range(2):
                    part = cf[s * SLICE + c * PART:s * SLICE + (c + 1) * PART, e * HS:(e + 1) * HS]
                    cl[c, e, s] = jnp.concatenate([part, jnp.zeros((8, HS), F32)], axis=0).astype(BF)

    def part_copy(k, e, s):
        to = (ctx + k) % 8
        return send(
            cl.at[to, e, s], crl.at[xlo * 2 + core, ctx], cl_s.at[0 if k else 1], cl_r, dp=s * 4 + y, ctx=to, mod=e
        )

    def send_parts():
        for k in (4, 5, 7, 6, 1, 3, 2):
            for e in range(2):
                for s in range(2):
                    part_copy(k, e, s).start()
        for e in range(2):
            for s in range(2):
                own = jnp.logical_and(xlo == s, core == e)

                @pl.when(own)
                def _():
                    pltpu.make_async_copy(cl.at[ctx, e, s], crl.at[xlo * 2 + core, ctx], cl_r).start()

                @pl.when(jnp.logical_not(own))
                def _():
                    part_copy(0, e, s).start()

    def finish(slot, totals):
        for e, total in enumerate(totals):
            for s in range(2):
                padded = jnp.concatenate([total[s * PART:(s + 1) * PART], jnp.zeros((8, HS), F32)], axis=0)
                fin[slot, s, e] = padded.astype(BF)

    def last_leg(slot):
        arrived(cxr.at[slot], cx_r.at[slot, 0])
        second = keep[slot, 1]
        arrived(czr.at[slot], cx_r.at[slot, 1])
        for k in range(3):
            second += czr[slot, k].astype(F32)
        finish(slot, [keep[slot, 0] + cxr[slot].astype(F32), second])

    def each(step):
        def run(slot, carry):
            step(slot)
            return carry

        return run

    lax.fori_loop(0, 3, two_heads, 0)
    rest_of_head(3, head_scores(3))
    spread_grads(3, 0, 3)

    for c in range(8):
        for i in range(2):
            dkvb[i, c // 4, c % 4] = acc[i, :, c * CHIP:(c + 1) * CHIP].astype(BF)
    copies = [send(dkvb.at[1, 1 - xhi], dvr, dk_s.at[0], dk_r.at[0], ctx=xctx)]
    for k in (1, 3, 2):
        to = (z + k) % 4
        copies.append(send(dkvb.at[0, :, to], dkr.at[k - 1], dk_s.at[1], dk_r.at[1], ctx=xhi * 4 + to))
    for copy in copies:
        copy.start()


    @pl.when(home)
    def _():
        for i in (2, 3):
            relay_grads(i)

    arrived(attf.at[:, pl.ds(aligned(other, GW), GW)], att_r)
    att_out = pltpu.make_async_copy(attf, att_o, w_sem.at[7])
    att_out.start()
    arrived(gq.at[:, pl.ds(aligned(other, GW), GW)], gq_r)

    def spread(i, carry):
        rows = pl.ds(aligned(i, 512), 512)
        total = dot(gq[...], wq_v[rows, :], ((1,), (1,)))
        high = total.astype(BF)
        hidf[:, rows] = high
        sb[:, rows] = (total - high.astype(F32)).astype(BF)
        return carry

    lax.fori_loop(0, 7, spread, 0)

    @pl.when(home)
    def _():
        for i in (4, 5, 6):
            relay_grads(i)

    arrived(at.at[:, 0:8 * BLOCK], af_r)
    other_kinds()

    def block_and_legs(slot):
        block_sums(slot)
        first_leg(slot)

    lax.fori_loop(core // 2, 1, each(block_sums), 0)

    copies[0].wait_recv()
    for k in (1, 3, 2):
        to = (z + k) % 4
        lanes = pl.ds(pl.multiple_of((xhi * 4 + to) * CHIP, CHIP), CHIP)
        dvz[to] = (acc[1, :, lanes] + dvr[to].astype(F32)).astype(BF)
        copy = send(dvz.at[to], dvzr.at[k - 1], dk_s.at[0], dk_r.at[2], ctx=xhi * 4 + to)
        copy.start()
    arrived(dkr, dk_r.at[1])

    def over_z(half):
        total = acc[0, :, pl.ds(pl.multiple_of((half * 4 + z) * CHIP, CHIP), CHIP)]
        for k in range(3):
            total += dkr[k, half].astype(F32)
        return total

    dkx[...] = over_z(1 - xhi).astype(BF)
    dk_copy = send(dkx, dkxr, dk_s.at[0], dk_r.at[3], ctx=xctx)
    dk_copy.start()
    first_leg(0)
    lax.fori_loop(1 + core // 2, 2, each(block_and_legs), 0)
    dk = over_z(xhi)
    dv = acc[1, :, pl.ds(pl.multiple_of((xhi * 4 + z) * CHIP, CHIP), CHIP)] + dvr[z].astype(F32)
    arrived(dvzr, dk_r.at[2])
    for k in range(3):
        dv += dvzr[k].astype(F32)
    gkv[1, core] = dv.T.astype(BF)
    dk_copy.wait_recv()
    dk = (dk + dkxr[...].astype(F32)) * scale
    gkv[0, core] = dk.T.astype(BF)
    gkv_copy = send(gkv.at[:, core], gkv.at[:, core], pair_s.at[4], pair_r.at[4], mod=other)
    gkv_copy.start()
    sent.append(gkv_copy)

    @pl.when(jnp.logical_not(home))
    def _():
        cross_kv().start()

    @pl.when(home)
    def _():
        for i, target, slot in ((0, 0, 4), (1, 1, 3)):
            fan_out(gkv.at[i, core], xlo, target, slot, b_s.at[2])

    lax.fori_loop(2, last - 1, each(block_and_legs), 0)

    @pl.when(home)
    def _():
        arrived(gkvx, kx.at[1])
        for i, target, slot in ((0, 0, 4), (1, 1, 3)):
            fan_out(gkvx.at[i], 1 - xlo, target, slot, b_s.at[2])

    arrived(gkv.at[:, other], pair_r.at[4])
    grads_kv = jnp.concatenate([gkv[0, 0], gkv[0, 1], gkv[1, 0], gkv[1, 1]], axis=1)
    for i in range(7):
        rows = slice(i * 512, (i + 1) * 512)
        total = hidf[:, rows].astype(F32) + sb[:, rows].astype(F32) + dot(grads_kv, wkv_v[rows, :], ((1,), (1,)))
        sb[:, rows] = total.astype(BF)
    home_copy = send(sb.at[other_rows], sr, pair_s.at[5], pair_r.at[5], mod=other)
    home_copy.start()
    sent.append(home_copy)
    lax.fori_loop(core // 2, last - 1, each(second_leg), 0)
    lax.fori_loop(last - 1, last, each(products), 0)
    straight_parts()
    send_parts()
    arrived(sr, pair_r.at[5])
    pick = jnp.broadcast_to(mods[here][0:1, 0:1], (BLOCK, D)) == expert
    ghf[...] = jnp.where(pick, sb[own_rows, :], sr[...])
    gh_out = pltpu.make_async_copy(ghf, gh_o, w_sem.at[8])
    gh_out.start()

    def results_out(slot):
        for s in range(2):
            for e in range(2):
                at_home = jnp.logical_and(xlo == s, core == e)

                @pl.when(at_home)
                def _():
                    pltpu.make_async_copy(
                        fin.at[slot, s, e], finr.at[xlo, core, slot], fin_r.at[core]
                    ).start()

                @pl.when(jnp.logical_not(at_home))
                def _():
                    result_copy(slot, s, e).start()

    def result_copy(slot, s, e):
        return send(
            fin.at[slot, s, e], finr.at[xlo, core, slot], fin_s.at[slot], fin_r.at[core],
            dp=s * 4 + y, mod=e,
        )

    def last_step(slot):
        last_leg(slot)
        results_out(slot)

    lax.fori_loop(core // 2, last - 1, each(last_step), 0)

    att_out.wait()
    gh_out.wait()
    arrived(finr.at[:, 0, 0:4], fin_r.at[0])
    arrived(finr.at[:, 1, 0:3], fin_r.at[1])
    arrived(crl, cl_r)
    for g in range(2):
        for c in range(2):
            total = crl[g * 2 + c, 0].astype(F32)
            for source in range(1, 8):
                total += crl[g * 2 + c, source].astype(F32)
            finr[g, c, 4 - c] = total.astype(BF)

    for copy in sent:
        copy.wait_send()

    arrived(attf.at[:, 0:GW], att_s)
    arrived(gq.at[:, 0:GW], gq_s)
    arrived(mods.at[0:15], mod_s)
    arrived(kvall.at[:, 0:7 * CHIP], kv_s)
    arrived(at.at[:, 0:8 * BLOCK], af_s)
    arrived(at.at[:, 0:7 * BLOCK], a_s)
    arrived(dkvb.at[0], dk_s.at[0])
    arrived(dkr, dk_s.at[1])

    @pl.when(jnp.logical_not(home))
    def _():
        arrived(dqb, bx_s)
        arrived(gkvx, kx.at[0])

    @pl.when(home)
    def _():
        arrived(bg.at[0:2, 0:7 * CHIP], b_s.at[2])
        for side in range(2):
            @pl.when(core == 0)
            def _():
                arrived(bg.at[0:3], b_s.at[side])

            @pl.when(core == 1)
            def _():
                arrived(bg.at[:, 0:5 * CHIP], b_s.at[side])

    def blocks_sent(slot, carry):
        arrived(cs.at[:, 0], c_s.at[slot])
        arrived(cz.at[slot], cx_s.at[slot])
        arrived(finr.at[0, 0, 0:3], fin_s.at[slot])
        return carry

    lax.fori_loop(0, last - 1, blocks_sent, 0)
    arrived(cl.at[0:7], cl_s.at[0])
    arrived(finr.at[0, 0, 0:3], cl_s.at[1])


def results(att, gh, fin, att_o, gh_o, gwq_o, gwkv_o):
    att_o[...] = att[...]
    gh_o[...] = gh[...]
    for g in range(2):
        for head in range(HEADS):
            cols = slice((g * HEADS + head) * HS, (g * HEADS + head + 1) * HS)
            gwq_o[:, cols] = fin[g, head // 4, head % 4][:PART]
        gwkv_o[:, g * HS:(g + 1) * HS] = fin[g, 0, 4][:PART]
        gwkv_o[:, KW + g * HS:KW + (g + 1) * HS] = fin[g, 1, 3][:PART]


def on_device(hidden_in, out_grad, modality, segment, w_query, w_keyval):
    vmem, dma = pltpu.VMEM, pltpu.SemaphoreType.DMA
    scratch = [
        vmem((BLOCK, D), BF), vmem((BLOCK, QW), BF), vmem((1, BLOCK), jnp.int32), vmem((1, SEQ), jnp.int32),
        vmem((BLOCK, QW), BF), vmem((BLOCK, D), BF), vmem((D, QW), BF), vmem((D, 2 * KW), BF),
        vmem((CHIP, D), BF), vmem((D, BLOCK), BF), vmem((CHIP, GW), BF), vmem((16, 8, HS), F32),
        vmem((2 * SLICE, SEQ), BF),
        vmem((2, 2, CHIP, HS), BF), vmem((2, CHIP, HS), BF), vmem((2, SEQ, HS), BF),
        vmem((2, CHIP, GW), BF), vmem((CHIP, GW), BF), vmem((CHIP, GW), BF), vmem((CHIP, SEQ), F32),
        vmem((8, BLOCK), F32), vmem((HEADS, CHIP, HS), BF), vmem((HEADS, CHIP, HS), BF), vmem((HEADS, CHIP, HS), BF), vmem((CHIP, QW), BF),
        vmem((2, HS, SEQ), F32), vmem((2, 2, 4, HS, CHIP), BF), vmem((3, 2, HS, CHIP), BF), vmem((4, HS, CHIP), BF), vmem((4, HS, CHIP), BF), vmem((3, HS, CHIP), BF),
        vmem((HS, CHIP), BF), vmem((HS, CHIP), BF), vmem((2, 2, CHIP, HS), BF), vmem((2, CHIP, HS), BF),
        vmem((5, SEQ, HS), BF), vmem((SEQ, 2 * HS), BF), vmem((2 * SLICE, 2 * HS), F32),
        vmem((5, 4, 2, 2 * PART, HS), BF), vmem((5, 4, 2, 2 * PART, HS), BF), vmem((5, 3, 2, 2 * PART, HS), BF), vmem((5, 4, 2 * PART, HS), BF),
        vmem((5, 2 * PART, HS), BF), vmem((5, 2 * PART, HS), BF), vmem((5, 4, 2 * PART, HS), BF), vmem((5, 3, 2 * PART, HS), BF), vmem((8, 2, 2, 64, HS), BF), vmem((4, 8, 64, HS), BF), vmem((5, 2, 2 * PART, HS), F32),
        vmem((5, 2, 2, 64, HS), BF),
        vmem((CHIP, D), BF), vmem((BLOCK, D), BF),
        dma((11,)), dma((6,)), dma((6,)), dma(()), dma((2,)), dma(()), dma((2, 4)), dma(()), dma(()),
        dma(()), dma((3,)), dma(()), dma(()), dma(()), dma(()),
        dma(()), dma((HEADS,)), dma((2,)), dma((3,)), dma((5,)), dma((2,)), dma((4,)), dma((5,)), dma((5, 2)), dma((5,)), dma((5, 2)),
        dma((2,)), dma(()), dma((5,)), dma((2,)),
    ]
    in_vmem, anywhere = pl.BlockSpec(memory_space=pltpu.VMEM), pl.BlockSpec(memory_space=pl.ANY)
    raw = pl.pallas_call(
        layer,
        out_shape=(
            jax.ShapeDtypeStruct((BLOCK, QW), BF),
            jax.ShapeDtypeStruct((BLOCK, D), BF),
            jax.ShapeDtypeStruct((2, 2, 5, 64, HS), BF),
        ),
        in_specs=[anywhere] * 6,
        out_specs=(anywhere, anywhere, in_vmem),
        scratch_shapes=scratch,
        compiler_params=pltpu.CompilerParams(
            collective_id=0, has_side_effects=True, vmem_limit_bytes=63 * 2**20
        ),
        name="layer",
    )(hidden_in[0], out_grad[0], modality, segment, w_query[0], w_keyval[0])
    attended, grad_hidden, grad_wq, grad_wkv = pl.pallas_call(
        results,
        out_shape=(
            jax.ShapeDtypeStruct((BLOCK, QW), BF),
            jax.ShapeDtypeStruct((BLOCK, D), BF),
            jax.ShapeDtypeStruct((PART, QW), BF),
            jax.ShapeDtypeStruct((PART, 2 * KW), BF),
        ),
        in_specs=[in_vmem] * 3,
        out_specs=(in_vmem,) * 4,
        name="results",
    )(*raw)
    return attended[None], grad_hidden[None], grad_wq[None], grad_wkv[None]


def solution(mesh):
    return jax.shard_map(
        on_device,
        mesh=mesh,
        in_specs=(
            P("dp", ("ctx", "mod"), None),
            P("dp", ("ctx", "mod"), None),
            P("dp", ("ctx", "mod")),
            P("dp", None),
            P("mod", None, None),
            P("mod", None, None),
        ),
        out_specs=(
            P("dp", ("ctx", "mod"), None),
            P("dp", ("ctx", "mod"), None),
            P("mod", ("dp", "ctx"), None),
            P("mod", ("dp", "ctx"), None),
        ),
        check_vma=False,
    )
```

```python
import functools
import math

import jax
import jax.numpy as jnp
from jax import lax
from jax.experimental import pallas as pl
from jax.experimental.pallas import tpu as pltpu
from jax.sharding import PartitionSpec as P

HS = 128
BLOCK = 128
D = 3584
QW = 1792
KW = 256
SEQ = 2048
HEADS = 7
GW = HEADS * HS
CHIP = 2 * BLOCK
SLICE = 448
PART = 56
MESH = pl.DeviceIdType.MESH
BF = jnp.bfloat16
F32 = jnp.float32


def aligned(index, step):
    return pl.multiple_of(index * step, step)


def dot(a, b, dims=((1,), (0,))):
    return lax.dot_general(a, b, (dims, ((), ())), preferred_element_type=F32)


def send(src, dst, send_sem, recv_sem, **device):
    return pltpu.make_async_remote_copy(
        src_ref=src, dst_ref=dst, send_sem=send_sem, recv_sem=recv_sem,
        device_id=device, device_id_type=MESH,
    )


def arrived(dst, sem):
    pltpu.make_async_copy(dst, dst, sem).wait()


def layer(
    hid_h, og_h, kinds_h, segs_h, wq, wkv,
    att_o, gh_o, finr,
    hid, og, kinds, segs, attf, ghf, wq_v, wkv_v, hidf, hid_t, ogf, mods, at, kvs, kvr, kvall, qs, qr, qf, bias,
    modv, attb, dqb, dqx, gq, acc, dkvb, dkr, dvr, dvz, dvzr, dkx, dkxr, gkv, gkvx, bg, be, cf, cs, cs1, crz, crx, cx, cxr, cz, czr, cl, crl, keep, fin, sb, sr,
    w_sem, pair_s, pair_r, mod_s, mod_r, a_s, a_r, af_s, af_r, kv_s, kv_r,
    att_s, att_r, gq_s, gq_r, bx_s, bx_r, kx, b_s, b_r, dk_s, dk_r, c_s, c_r, cx_s, cx_r, cl_s, cl_r, fin_s, fin_r,
):
    dp, ctx, core = lax.axis_index("dp"), lax.axis_index("ctx"), lax.axis_index("mod")
    xlo, y, xhi, z = dp // 4, dp % 4, ctx // 4, ctx % 4
    other = 1 - core
    here = dp * 2 + core
    expert = core.astype(F32)
    scale = 1.0 / math.sqrt(HS)

    q_cols = []
    for group in (other, core):
        for first, width in ((0, 512), (512, 384)):
            q_cols.append((group, first, width))
    own_loads = [
        pltpu.make_async_copy(hid_h, hid, w_sem.at[5]), pltpu.make_async_copy(og_h, og, w_sem.at[6]),
        pltpu.make_async_copy(kinds_h, kinds, w_sem.at[9]), pltpu.make_async_copy(segs_h, segs, w_sem.at[10]),
    ]
    loads = [pltpu.make_async_copy(wkv, wkv_v, w_sem.at[0])]
    for i, (group, first, width) in enumerate(q_cols):
        cols = pl.ds(pl.multiple_of(group * GW + first, 128), width)
        loads.append(pltpu.make_async_copy(wq.at[:, cols], wq_v.at[:, cols], w_sem.at[1 + i]))
    barrier = pltpu.get_barrier_semaphore()
    for k in range(8):
        pl.semaphore_signal(barrier, inc=1, device_id={"dp": (dp + k) % 8, "mod": other}, device_id_type=MESH)
        if k:
            pl.semaphore_signal(barrier, inc=1, device_id={"dp": (dp + k) % 8}, device_id_type=MESH)
            for side in range(2):
                for c in range(2):
                    to = {"dp": (1 - xlo if side else xlo) * 4 + y, "ctx": (ctx + k) % 8, "mod": other if c else core}
                    pl.semaphore_signal(barrier, inc=1, device_id=to, device_id_type=MESH)
    for load in own_loads + loads:
        load.start()
    for load in own_loads:
        load.wait()
    pl.semaphore_wait(barrier, 43)

    own_rows = pl.ds(aligned(core, BLOCK), BLOCK)
    other_rows = pl.ds(aligned(other, BLOCK), BLOCK)
    sent = []

    hid_copy = send(hid, hidf.at[own_rows], pair_s.at[0], pair_r.at[0], mod=other)
    hid_copy.start()
    og_copy = send(og.at[:, pl.ds(aligned(other, GW), GW)], ogf.at[own_rows], pair_s.at[1], pair_r.at[1], mod=other)
    og_copy.start()
    sent += [hid_copy, og_copy]
    modv[...] = jnp.broadcast_to(kinds[...].astype(F32), (8, BLOCK))
    mods[here] = modv[...]
    for k in range(8):
        for c in range(2):
            if k == 0 and c == 0:
                continue
            dev = {"dp": (dp + k) % 8, "mod": other if c else core}
            copy = send(modv, mods.at[here], mod_s, mod_r.at[1 if k else 0], **dev)
            copy.start()
    hidf[own_rows, :] = hid[...]
    ogf[own_rows, :] = og[:, pl.ds(aligned(core, GW), GW)]

    here_lanes = pl.ds(aligned(here, BLOCK), BLOCK)
    for i in range(7):
        hid_t[i * 512:(i + 1) * 512, :] = hid[:, i * 512:(i + 1) * 512].T
    def hidden_copy(side, k, s):
        to = (y + k) % 4
        rows = pl.ds(pl.multiple_of((s * 4 + to) * SLICE, 64), SLICE)
        return send(
            hid_t.at[rows], at.at[pl.ds(s * SLICE, SLICE), here_lanes], a_s, a_r.at[side],
            dp=(xlo if side == 0 else 1 - xlo) * 4 + to,
        )

    def send_hidden(side, k):
        for s in range(2):
            hidden_copy(side, k, s).start()

    for side, k in ((1, 0), (0, 1), (0, 3), (0, 2)):
        send_hidden(side, k)
    for s in range(2):
        rows = pl.ds(pl.multiple_of((s * 4 + y) * SLICE, 64), SLICE)
        at[s * SLICE:(s + 1) * SLICE, here_lanes] = hid_t[rows, :]

    def lanes_of(side, k):
        return pl.ds(pl.multiple_of((((xlo if side == 0 else 1 - xlo) * 4 + (y - k + 4) % 4) * 2 + core) * BLOCK, BLOCK), BLOCK)

    def pass_hidden(side, k):
        lanes = lanes_of(side, k)
        return send(at.at[:, lanes], at.at[:, lanes], af_s, af_r, mod=other)

    def relay_hidden(side, k):
        pass_hidden(side, k).start()

    loads[0].wait()

    def key_rows(rows):
        made = dot(hidf[rows, :], wkv_v[...]).astype(BF)
        for i in range(2):
            for g in range(2):
                kvs[i, g, rows, :] = made[:, (i * 2 + g) * HS:(i * 2 + g + 1) * HS]

    key_rows(own_rows)
    hid_copy.wait_recv()
    key_rows(other_rows)
    copy = send(kvs.at[:, other], kvr, pair_s.at[2], pair_r.at[2], mod=other)
    copy.start()
    sent.append(copy)
    def other_kinds():
        arrived(mods.at[0:14], mod_r.at[1])

    arrived(mods.at[dp * 2 + other], mod_r.at[0])
    mine = [
        jnp.broadcast_to(mods[dp * 2 + b][0:1, :], (BLOCK, HS)) == expert for b in range(2)
    ]
    copy.wait_recv()
    for i in range(2):
        for b in range(2):
            rows = slice(b * BLOCK, (b + 1) * BLOCK)
            kvall[i, pl.ds(pl.multiple_of(ctx * CHIP + b * BLOCK, BLOCK), BLOCK), :] = jnp.where(
                mine[b], kvs[i, core, rows, :], kvr[i, rows, :]
            )
    ctx_rows = pl.ds(aligned(ctx, CHIP), CHIP)
    xctx = (1 - xhi) * 4 + z
    xctx_rows = pl.ds(aligned(xctx, CHIP), CHIP)

    def rows_from(side, k):
        return pl.ds(aligned((xhi if side == 0 else 1 - xhi) * 4 + (z - k + 4) % 4, CHIP), CHIP)

    def send_keys(i, side, k, rows, to):
        copy = send(kvall.at[i, rows], kvall.at[i, rows], kv_s, kv_r.at[i if side and not k else 2], ctx=to)
        copy.start()

    def keys_from(i, side, k):
        arrived(kvall.at[i, rows_from(side, k)], kv_r.at[i])

    for i in range(2):
        send_keys(i, 1, 0, ctx_rows, xctx)
    for k in (1, 3, 2):
        for i in range(2):
            send_keys(i, 0, k, ctx_rows, xhi * 4 + (z + k) % 4)

    def project(i):
        group, first, width = q_cols[i]
        loads[1 + i].wait()
        cols = pl.ds(pl.multiple_of(group * GW + first, 128), width)
        qs[group, :, first:first + width] = dot(hidf[...], wq_v[:, cols]).astype(BF)

    project(0)
    for i in range(2):
        keys_from(i, 1, 0)
        for k in (1, 3, 2):
            send_keys(i, 1, k, xctx_rows, xhi * 4 + (z + k) % 4)
    for k in (2, 1, 3):
        send_hidden(1, k)
    project(1)
    q_copy = send(qs.at[other], qr, pair_s.at[3], pair_r.at[3], mod=other)
    q_copy.start()
    sent.append(q_copy)
    project(2)
    project(3)
    seg_rows = segs[:, pl.ds(aligned(ctx, CHIP), CHIP)].astype(F32)
    seg_col = jnp.broadcast_to(seg_rows, (128, CHIP)).T[:, 0:1]
    bias[...] = jnp.where(segs[...].astype(F32) <= seg_col, 0.0, -1e30)
    acc[...] = jnp.zeros_like(acc)
    q_copy.wait_recv()
    for b in range(2):
        rows = slice(b * BLOCK, (b + 1) * BLOCK)
        pick = jnp.broadcast_to(mods[dp * 2 + b][0:1, 0:1], (BLOCK, GW)) == expert
        qf[rows, :] = jnp.where(pick, qs[core, rows, :], qr[rows, :])
    og_copy.wait_recv()
    arrived(kvall.at[:, 0:6 * CHIP], kv_r.at[2])

    last = 5 - core

    def head_scores(head):
        q = qf[:, pl.ds(aligned(head, HS), HS)]
        return dot(q, kvall[0], ((1,), (1,))) * (scale * math.log2(math.e)) + bias[...]

    def rest_of_head(head, scores):
        lanes = pl.ds(aligned(head, HS), HS)
        full_lanes = pl.ds(aligned(core * HEADS + head, HS), HS)
        q, go = qf[:, lanes], ogf[:, lanes]
        keys, values = kvall[0], kvall[1]
        top = jnp.max(scores, axis=1, keepdims=True)
        weights = jnp.exp2(scores - top)
        total = jnp.sum(weights, axis=1, keepdims=True)
        low = weights.astype(BF)
        inv = 1.0 / total
        attended = (dot(low, values) * inv).astype(BF)
        attb[head] = attended
        copy = send(
            attb.at[head, other_rows], attf.at[:, full_lanes], att_s, att_r, mod=other
        )
        copy.start()
        attf[:, full_lanes] = attb[head, own_rows, :]
        go32 = go.astype(F32)
        delta = jnp.sum(go32 * attended.astype(F32), axis=1, keepdims=True)
        dprob = dot(go, values, ((1,), (1,)))
        dscore = (weights * (dprob * inv - delta * inv)).astype(BF)
        dq = (dot(dscore, keys) * scale).astype(BF)
        dqb[head] = dq
        gq[:, full_lanes] = dq
        copy = send(dqb.at[head], gq.at[:, full_lanes], gq_s, gq_r, mod=other)
        copy.start()
        acc[0] += dot(q.T, dscore)
        acc[1] += dot((go32 * inv).astype(BF).T, low)

    def two_heads(p, carry):
        first, second = head_scores(p), head_scores(4 + p)
        rest_of_head(p, first)
        rest_of_head(4 + p, second)
        spread_grads(p, 0, p)
        spread_grads(4 + p, 1, p)

        @pl.when(jnp.logical_and(home, p == 2))
        def _():
            arrived(dqx.at[0:2], bx_r.at[0])
            relay_grads(0)
            relay_grads(1)

        @pl.when(p == 1)
        def _():
            arrived(at.at[:, 0:3 * BLOCK], a_r.at[0])
            for k in range(4):
                relay_hidden(0, k)

        @pl.when(p == 2)
        def _():
            arrived(at.at[:, 0:4 * BLOCK], a_r.at[1])
            for k in (0, 2, 1, 3):
                relay_hidden(1, k)

        return carry

    home = xlo == core

    def cross(head):
        return send(dqb.at[head], dqx.at[head], bx_s, bx_r.at[head % 4 - head % 4 // 3], dp=(1 - xlo) * 4 + y)

    def cross_kv():
        return send(gkv.at[:, core], gkvx, kx.at[0], kx.at[1], dp=(1 - xlo) * 4 + y)

    def fan(src, side, target, slot, sems, k):
        rows = pl.ds(pl.multiple_of((side * 4 + y) * CHIP, CHIP), CHIP)
        return send(
            src, bg.at[slot, rows], sems, b_r.at[slot], dp=xlo * 4 + (y + k) % 4, mod=target
        )

    def fan_out(src, side, target, slot, sems):
        rows = pl.ds(pl.multiple_of((side * 4 + y) * CHIP, CHIP), CHIP)
        for k in (1, 3, 2):
            fan(src, side, target, slot, sems, k).start()

        @pl.when(target == core)
        def _():
            pltpu.make_async_copy(src, bg.at[slot, rows], b_r.at[slot]).start()

        @pl.when(target != core)
        def _():
            fan(src, side, target, slot, sems, 0).start()

    def relay_grads(i):
        slot, target = i // 2, i % 2
        head = target * 4 + slot
        fan_out(dqx.at[head], 1 - xlo, target, slot, b_s.at[1])

    def spread_grads(head, target, slot):
        @pl.when(jnp.logical_not(home))
        def _():
            cross(head).start()

        @pl.when(home)
        def _():
            fan_out(dqb.at[head], xlo, target, slot, b_s.at[0])

    def products(slot):
        arrived(bg.at[slot], b_r.at[slot])
        for t in range(16):
            rows = slice(t * BLOCK, (t + 1) * BLOCK)
            kind = mods[t][0:1, :]
            block = bg[slot, rows, :]
            second = jnp.where(jnp.broadcast_to(kind, (BLOCK, HS)) == 1.0, block, jnp.zeros_like(block))
            be[rows, HS:] = second
            be[rows, :HS] = block - second
        cf[...] = dot(at[...], be[...])

    def block_sums(slot):
        products(slot)
        for c in range(8):
            for e, buf in enumerate((cs, cs1)):
                cols = slice(e * HS, (e + 1) * HS)
                both = jnp.concatenate(
                    [cf[c * PART:(c + 1) * PART, cols], cf[SLICE + c * PART:SLICE + (c + 1) * PART, cols]], axis=0
                )
                buf[slot, c % 4, c // 4] = both.astype(BF)

    def z_leg(slot, k):
        to = (z + k) % 4
        return send(cs.at[slot, to], crz.at[slot, k - 1], c_s.at[slot], c_r.at[slot, 1], ctx=xhi * 4 + to)

    def x_leg(slot):
        return send(cs1.at[slot, :, 1 - xhi], crx.at[slot], c_s.at[slot], c_r.at[slot, 0], ctx=xctx)

    def then_x(slot):
        return send(cx.at[slot], cxr.at[slot], cx_s.at[slot], cx_r.at[slot, 0], ctx=xctx)

    def then_z(slot, k):
        to = (z + k) % 4
        return send(cz.at[slot, to], czr.at[slot, k - 1], cx_s.at[slot], cx_r.at[slot, 1], ctx=xhi * 4 + to)

    def first_leg(slot):
        x_leg(slot).start()
        for k in (1, 3, 2):
            z_leg(slot, k).start()

    def second_leg(slot):
        arrived(crx.at[slot], c_r.at[slot, 0])
        for k in (1, 3, 2):
            to = (z + k) % 4
            cz[slot, to] = (cs1[slot, to, xhi].astype(F32) + crx[slot, to].astype(F32)).astype(BF)
            then_z(slot, k).start()
        keep[slot, 1] = cs1[slot, z, xhi].astype(F32) + crx[slot, z].astype(F32)
        arrived(crz.at[slot], c_r.at[slot, 1])
        total = cs[slot, z, 1 - xhi].astype(F32)
        for k in range(3):
            total += crz[slot, k, 1 - xhi].astype(F32)
        cx[slot] = total.astype(BF)
        then_x(slot).start()
        total = cs[slot, z, xhi].astype(F32)
        for k in range(3):
            total += crz[slot, k, xhi].astype(F32)
        keep[slot, 0] = total

    def straight_parts():
        for c in range(8):
            for e in range(2):
                for s in range(2):
                    part = cf[s * SLICE + c * PART:s * SLICE + (c + 1) * PART, e * HS:(e + 1) * HS]
                    cl[c, e, s] = jnp.concatenate([part, jnp.zeros((8, HS), F32)], axis=0).astype(BF)

    def part_copy(k, e, s):
        to = (ctx + k) % 8
        return send(
            cl.at[to, e, s], crl.at[xlo * 2 + core, ctx], cl_s.at[0 if k else 1], cl_r, dp=s * 4 + y, ctx=to, mod=e
        )

    def send_parts():
        for k in (4, 5, 7, 6, 1, 3, 2):
            for e in range(2):
                for s in range(2):
                    part_copy(k, e, s).start()
        for e in range(2):
            for s in range(2):
                own = jnp.logical_and(xlo == s, core == e)

                @pl.when(own)
                def _():
                    pltpu.make_async_copy(cl.at[ctx, e, s], crl.at[xlo * 2 + core, ctx], cl_r).start()

                @pl.when(jnp.logical_not(own))
                def _():
                    part_copy(0, e, s).start()

    def finish(slot, totals):
        for e, total in enumerate(totals):
            for s in range(2):
                padded = jnp.concatenate([total[s * PART:(s + 1) * PART], jnp.zeros((8, HS), F32)], axis=0)
                fin[slot, s, e] = padded.astype(BF)

    def last_leg(slot):
        arrived(cxr.at[slot], cx_r.at[slot, 0])
        second = keep[slot, 1]
        arrived(czr.at[slot], cx_r.at[slot, 1])
        for k in range(3):
            second += czr[slot, k].astype(F32)
        finish(slot, [keep[slot, 0] + cxr[slot].astype(F32), second])

    def each(step):
        def run(slot, carry):
            step(slot)
            return carry

        return run

    lax.fori_loop(0, 3, two_heads, 0)
    rest_of_head(3, head_scores(3))
    spread_grads(3, 0, 3)

    for c in range(8):
        for i in range(2):
            dkvb[i, c // 4, c % 4] = acc[i, :, c * CHIP:(c + 1) * CHIP].astype(BF)
    copies = [send(dkvb.at[1, 1 - xhi], dvr, dk_s.at[0], dk_r.at[0], ctx=xctx)]
    for k in (1, 3, 2):
        to = (z + k) % 4
        copies.append(send(dkvb.at[0, :, to], dkr.at[k - 1], dk_s.at[1], dk_r.at[1], ctx=xhi * 4 + to))
    for copy in copies:
        copy.start()


    @pl.when(home)
    def _():
        arrived(dqx.at[0:2], bx_r.at[1])
        for i in (2, 3):
            relay_grads(i)

    arrived(attf.at[:, pl.ds(aligned(other, GW), GW)], att_r)
    att_out = pltpu.make_async_copy(attf, att_o, w_sem.at[7])
    att_out.start()
    arrived(gq.at[:, pl.ds(aligned(other, GW), GW)], gq_r)

    def spread(i, carry):
        rows = pl.ds(aligned(i, 512), 512)
        total = dot(gq[...], wq_v[rows, :], ((1,), (1,)))
        high = total.astype(BF)
        hidf[:, rows] = high
        sb[:, rows] = (total - high.astype(F32)).astype(BF)
        return carry

    lax.fori_loop(0, 7, spread, 0)

    @pl.when(home)
    def _():
        arrived(dqx.at[0:3], bx_r.at[2])
        for i in (4, 5, 6):
            relay_grads(i)

    arrived(at.at[:, 0:8 * BLOCK], af_r)
    other_kinds()

    def block_and_legs(slot):
        block_sums(slot)
        first_leg(slot)

    lax.fori_loop(core // 2, 1, each(block_sums), 0)

    copies[0].wait_recv()
    for k in (1, 3, 2):
        to = (z + k) % 4
        lanes = pl.ds(pl.multiple_of((xhi * 4 + to) * CHIP, CHIP), CHIP)
        dvz[to] = (acc[1, :, lanes] + dvr[to].astype(F32)).astype(BF)
        copy = send(dvz.at[to], dvzr.at[k - 1], dk_s.at[0], dk_r.at[2], ctx=xhi * 4 + to)
        copy.start()
    arrived(dkr, dk_r.at[1])

    def over_z(half):
        total = acc[0, :, pl.ds(pl.multiple_of((half * 4 + z) * CHIP, CHIP), CHIP)]
        for k in range(3):
            total += dkr[k, half].astype(F32)
        return total

    dkx[...] = over_z(1 - xhi).astype(BF)
    dk_copy = send(dkx, dkxr, dk_s.at[0], dk_r.at[3], ctx=xctx)
    dk_copy.start()
    first_leg(0)
    lax.fori_loop(1 + core // 2, 2, each(block_and_legs), 0)
    dk = over_z(xhi)
    dv = acc[1, :, pl.ds(pl.multiple_of((xhi * 4 + z) * CHIP, CHIP), CHIP)] + dvr[z].astype(F32)
    arrived(dvzr, dk_r.at[2])
    for k in range(3):
        dv += dvzr[k].astype(F32)
    gkv[1, core] = dv.T.astype(BF)
    dk_copy.wait_recv()
    dk = (dk + dkxr[...].astype(F32)) * scale
    gkv[0, core] = dk.T.astype(BF)
    gkv_copy = send(gkv.at[:, core], gkv.at[:, core], pair_s.at[4], pair_r.at[4], mod=other)
    gkv_copy.start()
    sent.append(gkv_copy)

    @pl.when(jnp.logical_not(home))
    def _():
        cross_kv().start()

    @pl.when(home)
    def _():
        for i, target, slot in ((0, 0, 4), (1, 1, 3)):
            fan_out(gkv.at[i, core], xlo, target, slot, b_s.at[2])

    lax.fori_loop(2, last - 1, each(block_and_legs), 0)

    @pl.when(home)
    def _():
        arrived(gkvx, kx.at[1])
        for i, target, slot in ((0, 0, 4), (1, 1, 3)):
            fan_out(gkvx.at[i], 1 - xlo, target, slot, b_s.at[2])

    arrived(gkv.at[:, other], pair_r.at[4])
    grads_kv = jnp.concatenate([gkv[0, 0], gkv[0, 1], gkv[1, 0], gkv[1, 1]], axis=1)
    for i in range(7):
        rows = slice(i * 512, (i + 1) * 512)
        total = hidf[:, rows].astype(F32) + sb[:, rows].astype(F32) + dot(grads_kv, wkv_v[rows, :], ((1,), (1,)))
        sb[:, rows] = total.astype(BF)
    home_copy = send(sb.at[other_rows], sr, pair_s.at[5], pair_r.at[5], mod=other)
    home_copy.start()
    sent.append(home_copy)
    lax.fori_loop(core // 2, last - 1, each(second_leg), 0)
    lax.fori_loop(last - 1, last, each(products), 0)
    straight_parts()
    send_parts()
    arrived(sr, pair_r.at[5])
    pick = jnp.broadcast_to(mods[here][0:1, 0:1], (BLOCK, D)) == expert
    ghf[...] = jnp.where(pick, sb[own_rows, :], sr[...])
    gh_out = pltpu.make_async_copy(ghf, gh_o, w_sem.at[8])
    gh_out.start()

    def results_out(slot):
        for s in range(2):
            for e in range(2):
                at_home = jnp.logical_and(xlo == s, core == e)

                @pl.when(at_home)
                def _():
                    pltpu.make_async_copy(
                        fin.at[slot, s, e], finr.at[xlo, core, slot], fin_r.at[core]
                    ).start()

                @pl.when(jnp.logical_not(at_home))
                def _():
                    result_copy(slot, s, e).start()

    def result_copy(slot, s, e):
        return send(
            fin.at[slot, s, e], finr.at[xlo, core, slot], fin_s.at[slot], fin_r.at[core],
            dp=s * 4 + y, mod=e,
        )

    def last_step(slot):
        last_leg(slot)
        results_out(slot)

    lax.fori_loop(core // 2, last - 1, each(last_step), 0)

    att_out.wait()
    gh_out.wait()
    arrived(finr.at[:, 0, 0:4], fin_r.at[0])
    arrived(finr.at[:, 1, 0:3], fin_r.at[1])
    arrived(crl, cl_r)
    for g in range(2):
        for c in range(2):
            total = crl[g * 2 + c, 0].astype(F32)
            for source in range(1, 8):
                total += crl[g * 2 + c, source].astype(F32)
            finr[g, c, 4 - c] = total.astype(BF)

    for copy in sent:
        copy.wait_send()

    arrived(attf.at[:, 0:GW], att_s)
    arrived(gq.at[:, 0:GW], gq_s)
    arrived(mods.at[0:15], mod_s)
    arrived(kvall.at[:, 0:7 * CHIP], kv_s)
    arrived(at.at[:, 0:8 * BLOCK], af_s)
    arrived(at.at[:, 0:7 * BLOCK], a_s)
    arrived(dkvb.at[0], dk_s.at[0])
    arrived(dkr, dk_s.at[1])

    @pl.when(jnp.logical_not(home))
    def _():
        arrived(dqb, bx_s)
        arrived(gkvx, kx.at[0])

    @pl.when(home)
    def _():
        arrived(bg.at[0:2, 0:7 * CHIP], b_s.at[2])
        for side in range(2):
            @pl.when(core == 0)
            def _():
                arrived(bg.at[0:3], b_s.at[side])

            @pl.when(core == 1)
            def _():
                arrived(bg.at[:, 0:5 * CHIP], b_s.at[side])

    def blocks_sent(slot, carry):
        arrived(cs.at[:, 0], c_s.at[slot])
        arrived(cz.at[slot], cx_s.at[slot])
        arrived(finr.at[0, 0, 0:3], fin_s.at[slot])
        return carry

    lax.fori_loop(0, last - 1, blocks_sent, 0)
    arrived(cl.at[0:7], cl_s.at[0])
    arrived(finr.at[0, 0, 0:3], cl_s.at[1])


def results(att, gh, fin, att_o, gh_o, gwq_o, gwkv_o):
    att_o[...] = att[...]
    gh_o[...] = gh[...]
    for g in range(2):
        for head in range(HEADS):
            cols = slice((g * HEADS + head) * HS, (g * HEADS + head + 1) * HS)
            gwq_o[:, cols] = fin[g, head // 4, head % 4][:PART]
        gwkv_o[:, g * HS:(g + 1) * HS] = fin[g, 0, 4][:PART]
        gwkv_o[:, KW + g * HS:KW + (g + 1) * HS] = fin[g, 1, 3][:PART]


def on_device(hidden_in, out_grad, modality, segment, w_query, w_keyval):
    vmem, dma = pltpu.VMEM, pltpu.SemaphoreType.DMA
    scratch = [
        vmem((BLOCK, D), BF), vmem((BLOCK, QW), BF), vmem((1, BLOCK), jnp.int32), vmem((1, SEQ), jnp.int32),
        vmem((BLOCK, QW), BF), vmem((BLOCK, D), BF), vmem((D, QW), BF), vmem((D, 2 * KW), BF),
        vmem((CHIP, D), BF), vmem((D, BLOCK), BF), vmem((CHIP, GW), BF), vmem((16, 8, HS), F32),
        vmem((2 * SLICE, SEQ), BF),
        vmem((2, 2, CHIP, HS), BF), vmem((2, CHIP, HS), BF), vmem((2, SEQ, HS), BF),
        vmem((2, CHIP, GW), BF), vmem((CHIP, GW), BF), vmem((CHIP, GW), BF), vmem((CHIP, SEQ), F32),
        vmem((8, BLOCK), F32), vmem((HEADS, CHIP, HS), BF), vmem((HEADS, CHIP, HS), BF), vmem((HEADS, CHIP, HS), BF), vmem((CHIP, QW), BF),
        vmem((2, HS, SEQ), F32), vmem((2, 2, 4, HS, CHIP), BF), vmem((3, 2, HS, CHIP), BF), vmem((4, HS, CHIP), BF), vmem((4, HS, CHIP), BF), vmem((3, HS, CHIP), BF),
        vmem((HS, CHIP), BF), vmem((HS, CHIP), BF), vmem((2, 2, CHIP, HS), BF), vmem((2, CHIP, HS), BF),
        vmem((5, SEQ, HS), BF), vmem((SEQ, 2 * HS), BF), vmem((2 * SLICE, 2 * HS), F32),
        vmem((5, 4, 2, 2 * PART, HS), BF), vmem((5, 4, 2, 2 * PART, HS), BF), vmem((5, 3, 2, 2 * PART, HS), BF), vmem((5, 4, 2 * PART, HS), BF),
        vmem((5, 2 * PART, HS), BF), vmem((5, 2 * PART, HS), BF), vmem((5, 4, 2 * PART, HS), BF), vmem((5, 3, 2 * PART, HS), BF), vmem((8, 2, 2, 64, HS), BF), vmem((4, 8, 64, HS), BF), vmem((5, 2, 2 * PART, HS), F32),
        vmem((5, 2, 2, 64, HS), BF),
        vmem((CHIP, D), BF), vmem((BLOCK, D), BF),
        dma((11,)), dma((6,)), dma((6,)), dma(()), dma((2,)), dma(()), dma((2,)), dma(()), dma(()),
        dma(()), dma((3,)), dma(()), dma(()), dma(()), dma(()),
        dma(()), dma((3,)), dma((2,)), dma((3,)), dma((5,)), dma((2,)), dma((4,)), dma((4,)), dma((4, 2)), dma((4,)), dma((4, 2)),
        dma((2,)), dma(()), dma((4,)), dma((2,)),
    ]
    in_vmem, anywhere = pl.BlockSpec(memory_space=pltpu.VMEM), pl.BlockSpec(memory_space=pl.ANY)
    raw = pl.pallas_call(
        layer,
        out_shape=(
            jax.ShapeDtypeStruct((BLOCK, QW), BF),
            jax.ShapeDtypeStruct((BLOCK, D), BF),
            jax.ShapeDtypeStruct((2, 2, 5, 64, HS), BF),
        ),
        in_specs=[anywhere] * 6,
        out_specs=(anywhere, anywhere, in_vmem),
        scratch_shapes=scratch,
        compiler_params=pltpu.CompilerParams(
            collective_id=0, has_side_effects=True, vmem_limit_bytes=63 * 2**20
        ),
        name="layer",
    )(hidden_in[0], out_grad[0], modality, segment, w_query[0], w_keyval[0])
    attended, grad_hidden, grad_wq, grad_wkv = pl.pallas_call(
        results,
        out_shape=(
            jax.ShapeDtypeStruct((BLOCK, QW), BF),
            jax.ShapeDtypeStruct((BLOCK, D), BF),
            jax.ShapeDtypeStruct((PART, QW), BF),
            jax.ShapeDtypeStruct((PART, 2 * KW), BF),
        ),
        in_specs=[in_vmem] * 3,
        out_specs=(in_vmem,) * 4,
        name="results",
    )(*raw)
    return attended[None], grad_hidden[None], grad_wq[None], grad_wkv[None]


def solution(mesh):
    return jax.shard_map(
        on_device,
        mesh=mesh,
        in_specs=(
            P("dp", ("ctx", "mod"), None),
            P("dp", ("ctx", "mod"), None),
            P("dp", ("ctx", "mod")),
            P("dp", None),
            P("mod", None, None),
            P("mod", None, None),
        ),
        out_specs=(
            P("dp", ("ctx", "mod"), None),
            P("dp", ("ctx", "mod"), None),
            P("mod", ("dp", "ctx"), None),
            P("mod", ("dp", "ctx"), None),
        ),
        check_vma=False,
    )
```
